128 devices in a mesh: outer: 8 (over y, core), inner: 16 (over z, x).
Axes of the slice: x: 4, y: 4, z: 4, core: 2. Of those that a mesh axis runs over, the one named last changes fastest.
Arguments:
- entities: float32 [262144, 400], P(('outer', 'inner')), may hold values from -0.3 to 0.3
- panel_rows: float32 [16384, 400], P(('outer', 'inner')), may hold values from -0.3 to 0.3
- relations: float32 [240, 400], replicated, may hold values from -2 to 2
- source_owner: int32 [131072], P(('outer', 'inner')), may hold values from 0 to 127, as said below
- source_row: int32 [131072], P(('outer', 'inner')), may hold values from 0 to 2047
- relation_ids: int32 [131072], P(('outer', 'inner')), may hold values from 0 to 239
- target_ids: int32 [131072], P(('outer', 'inner')), may hold values from 0 to 2047
- negatives: int32 [128, 1024], P(('outer', 'inner')), may hold values from 0 to 2047
Outputs:
- entity_grad: float32 [262144, 400], P(('outer', 'inner'))
- panel_grad: float32 [16384, 400], P(('outer', 'inner'))
- relation_grad: float32 [240, 400], replicated
The draws below stay inside these ranges and needn't reach their ends.
Inputs may be any that keep to these rules, and one draw needn't show every extreme that they name: `source_owner`: each device's edges name every device as owner at most 12 times; one device, the same for all, is named exactly 12 times by every device's edges.
All inputs are finite; a program needn't handle non-finite values.
Results may differ from the reference program's by a relative error of at most 0.0003.
Values sent between devices are 32-bit elements; how exact they have to be, the bound alone decides.
A program may use at most 128 MiB of HBM per device.

```python
import math
import jax
import jax.numpy as jnp
import numpy as np
from jax import lax

D = 400
R = 240
ROWS_DEV = 2048
PANEL_DEV = 128
E_DEV = 1024
BLOCK = 1024
NEG = 1024
BLOCKS = 1
CAP = 12
ENTITIES = 262144
PANELS = 16384
N_OUTER = 8
N_INNER = 16
DEVICES = 128


def draw_source_owner(key, part):
    key = jax.random.fold_in(key, 11)
    hottest = jax.random.randint(jax.random.fold_in(key, 1), (), 0, DEVICES)
    favour = jax.random.randint(jax.random.fold_in(key, 2), (DEVICES,), 0, 32768)
    device_keys = jax.random.split(jax.random.fold_in(key, 3), DEVICES)

    def one_device(device_key):
        score_key, order_key = jax.random.split(device_key)
        slots = jnp.arange(DEVICES * CAP, dtype=jnp.int32)
        owners = slots // CAP
        scores = jax.random.randint(score_key, (DEVICES * CAP,), 0, 32768) + favour[owners]
        scores = jnp.where(owners == hottest, 65536, scores)
        keyed = scores * 16384 + slots
        chosen = lax.top_k(keyed, E_DEV)[1].astype(jnp.int32)
        return jax.random.permutation(order_key, chosen // CAP)
    return jax.vmap(one_device)(device_keys).reshape(DEVICES * E_DEV).astype(jnp.int32)


def plant(drawn, rng, least, top_value):
    longest = drawn.shape.index(max(drawn.shape))
    spots = []
    for shift in (0, 1):
        where = [jax.random.randint(jax.random.fold_in(rng, axis), (), 0, length) for axis, length in enumerate(drawn.shape)]
        where[longest] = (where[longest] + shift) % drawn.shape[longest]
        spots.append(tuple(where))
    return drawn.at[spots[0]].set(least).at[spots[1]].set(top_value)


def level_of(rng, dims, cuts, low, top_value):
    level, own = 1.0, jax.random.fold_in(rng, 6)
    for axis_at, blocks in cuts:
        heights = jnp.exp(jax.random.uniform(jax.random.fold_in(own, axis_at), (blocks,), jnp.float32, low / len(cuts), top_value / len(cuts)))
        level = level * jnp.repeat(heights, dims[axis_at] // blocks).reshape([-1 if axis == axis_at else 1 for axis in range(len(dims))])
    return level


def rank_table(number_of, lean):
    loads = [(1 << 20) // math.isqrt(rank ** lean) + 1 for rank in range(1, number_of + 1)]
    width = 1 + sum(loads) // (1 << 30)
    return np.cumsum(np.array([max(1, weight // width) for weight in loads]))


def skewed_ids(rng, dims, count, slope):
    table = rank_table(count, slope)
    lot = jax.random.randint(jax.random.fold_in(rng, 1), dims, 0, int(table[count - 1]))
    rank = jnp.searchsorted(jnp.asarray(table, jnp.int32), lot, side="right")
    return jax.random.permutation(jax.random.fold_in(rng, 2), count)[rank].astype(jnp.int32)


def scatter_about(own_key, extent, scale, reach, cuts=(), kind=jnp.bfloat16):
    level = level_of(own_key, extent, cuts, -0.22, 0.18) if cuts else 1.0
    result = jax.random.normal(own_key, extent, jnp.float32) * scale * level
    return jnp.minimum(jnp.maximum(result, -reach), reach).astype(kind)


def setup_inputs(seed: int = 0) -> dict:
    splits = jax.random.split(jax.random.key(seed), 9)
    return {
        "entities": scatter_about(splits[0], (ENTITIES, D), 0.1, 0.3, ((0, 128),), jnp.float32),
        "panel_rows": scatter_about(splits[1], (PANELS, D), 0.1, 0.3, ((0, 128),), jnp.float32),
        "relations": jnp.clip(jax.random.uniform(splits[2], (R, D), jnp.float32, -2.0, 2.0), -2.0, 2.0),
        "source_owner": draw_source_owner(jax.random.fold_in(splits[8], 71), 0),
        "source_row": plant(jax.random.randint(splits[4], (DEVICES * E_DEV,), 0, ROWS_DEV), jax.random.fold_in(splits[4], 1), 0, ROWS_DEV - 1).astype(jnp.int32),
        "relation_ids": plant(skewed_ids(splits[5], (DEVICES * E_DEV,), R, 2), jax.random.fold_in(splits[5], 3), 0, R - 1).astype(jnp.int32),
        "target_ids": plant(skewed_ids(splits[6], (DEVICES * E_DEV,), N_INNER * PANEL_DEV, 1), jax.random.fold_in(splits[6], 3), 0, (N_INNER * PANEL_DEV) - 1).astype(jnp.int32),
        "negatives": plant(jax.random.randint(splits[7], (DEVICES * BLOCKS, NEG), 0, N_INNER * PANEL_DEV), jax.random.fold_in(splits[7], 1), 0, (N_INNER * PANEL_DEV) - 1).astype(jnp.int32),
    }


def block_grads(source_vecs, rel_scale, target_vecs, negative_vecs):
    query_vecs = source_vecs * rel_scale
    positive = jnp.sum(query_vecs * target_vecs, axis=1)
    scores = jnp.dot(query_vecs, negative_vecs.T, precision=lax.Precision.HIGHEST, preferred_element_type=jnp.float32)
    pos_exp = jnp.exp(positive)
    neg_exp = jnp.exp(scores)
    denominator = pos_exp + jnp.sum(neg_exp, axis=1)
    pos_weight = pos_exp / denominator - 1.0
    neg_weight = neg_exp / denominator[:, None]
    grad_query = pos_weight[:, None] * target_vecs + jnp.dot(neg_weight, negative_vecs, precision=lax.Precision.HIGHEST, preferred_element_type=jnp.float32)
    grad_negative = jnp.dot(neg_weight.T, query_vecs, precision=lax.Precision.HIGHEST, preferred_element_type=jnp.float32)
    grad_target = pos_weight[:, None] * query_vecs
    return grad_query, grad_negative, grad_target


def reference(entities, panel_rows, relations, source_owner, source_row, relation_ids, target_ids, negatives):
    devices = N_OUTER * N_INNER
    group_rows = N_INNER * PANEL_DEV

    def one_device(totals, device_index):
        ent_total, panel_total, rel_total = totals
        owner_ids = lax.dynamic_slice_in_dim(source_owner, device_index * E_DEV, E_DEV)
        row_ids = lax.dynamic_slice_in_dim(source_row, device_index * E_DEV, E_DEV)
        rel_ids = lax.dynamic_slice_in_dim(relation_ids, device_index * E_DEV, E_DEV)
        tgt_ids = lax.dynamic_slice_in_dim(target_ids, device_index * E_DEV, E_DEV)
        neg_ids = lax.dynamic_slice_in_dim(negatives, device_index * BLOCKS, BLOCKS, 0)
        global_ids = owner_ids * ROWS_DEV + row_ids
        offset = (device_index // N_INNER) * group_rows
        source_vecs = entities[global_ids]
        rel_scale = relations[rel_ids]
        target_vecs = panel_rows[offset + tgt_ids]
        negative_vecs = panel_rows[offset + neg_ids]
        grad_query, grad_negative, grad_target = lax.map(
            lambda pieces: block_grads(*pieces),
            (source_vecs.reshape(BLOCKS, BLOCK, D), rel_scale.reshape(BLOCKS, BLOCK, D),
             target_vecs.reshape(BLOCKS, BLOCK, D), negative_vecs))
        grad_query = grad_query.reshape(E_DEV, D)
        ent_total = ent_total.at[global_ids].add(grad_query * rel_scale)
        panel_total = panel_total.at[offset + tgt_ids].add(grad_target.reshape(E_DEV, D))
        panel_total = panel_total.at[offset + neg_ids.reshape(-1)].add(grad_negative.reshape(BLOCKS * NEG, D))
        rel_total = rel_total + jax.ops.segment_sum(grad_query * source_vecs, rel_ids, num_segments=R)
        return (ent_total, panel_total, rel_total), None

    start = (jnp.zeros((ENTITIES, D), jnp.float32), jnp.zeros((PANELS, D), jnp.float32), jnp.zeros((R, D), jnp.float32))
    finals, unused = lax.scan(one_device, start, jnp.arange(devices, dtype=jnp.int32))
    return finals[0], finals[1], finals[2]
```

```python
import jax
import jax.numpy as jnp
from jax import lax
from jax.experimental import pallas as pl
from jax.experimental.pallas import tpu as pltpu
from jax.sharding import PartitionSpec as P

MESH = pl.DeviceIdType.MESH
F32, BF16, I32 = jnp.float32, jnp.bfloat16, jnp.int32

D, DP = 400, 512
HALF = 200
RELS = 240
ROWS = 2048
PANEL = 128
EDGES = 1024
CAP = 12
NO, NI = 8, 16
DEV = NO * NI
SLOTS = CAP * DEV
MSG = 40
BM = 256

NN = (((1,), (0,)), ((), ()))
NT = (((1,), (1,)), ((), ()))


def dot(a, b, dims=NN):
    return lax.dot_general(a, b, dims, preferred_element_type=F32)


def split(x):
    hi = x.astype(BF16)
    return hi, (x - hi.astype(F32)).astype(BF16)


def iota(shape, dim):
    return lax.broadcasted_iota(I32, shape, dim)


def mark(cond):
    return jnp.where(cond, 1.0, 0.0).astype(BF16)


def step_kernel(
    ent_ref, pan_ref, rel_ref, owner_ref, srow_ref, rid_ref, tid_ref, neg_ref,
    eout_ref, pout_ref, rout_ref,
    entf, eh, el, want, tgt_t, rel_t, r1, s2, r2,
    pan_all, ph, plo, relh, rell, cnt,
    send_buf, fetched, returned, xs, gs, onehot, tcol, rcol,
    scores, wh, wl, acc, relacc,
    rsa1, rsb1, sa, sb, rsa2, rsb2,
    ra1, a1p, ra2, a3s, a3, c4,
    local_sem, all_in,
    i1s, i1r, i2s, i2r, g1s, g1r, g2s, g2r, fs, fr, bs, br,
    p1s, p1r, p2s, p2r, q1s, q1r, q2s, q2r, q3s, q3r, q4s, q4r,
):
    o, i = lax.axis_index("outer"), lax.axis_index("inner")
    me = o * NI + i
    mine = i * NO + o
    z, x = i >> 2, i & 3
    y, c = o >> 1, o & 1

    def outer_peer(d):
        return (o + d) & 7

    def inner_peer(d):
        return (i + d) & 15

    def xp(d):
        return (z << 2) + ((x + d) & 3)

    def zp(d):
        return (((z + d) & 3) << 2) + x

    def remote(src, dst, ss, rs, po, pi):
        return pltpu.make_async_remote_copy(
            src_ref=src, dst_ref=dst, send_sem=ss, recv_sem=rs,
            device_id=(po, pi), device_id_type=MESH,
        )

    barrier = pltpu.get_barrier_semaphore()

    def greet_outer(d, carry):
        pl.semaphore_signal(barrier, inc=1, device_id=(outer_peer(d), i), device_id_type=MESH)
        return carry

    def greet_inner(d, carry):
        pl.semaphore_signal(barrier, inc=1, device_id=(o, inner_peer(d)), device_id_type=MESH)
        return carry

    lax.fori_loop(1, NO, greet_outer, 0)
    lax.fori_loop(1, NI, greet_inner, 0)
    load = pltpu.make_async_copy(ent_ref, entf, local_sem.at[0])
    load.start()

    owner = owner_ref[...]
    owned = owner == iota((DEV, EDGES), 0)
    owned_b = mark(owned)
    before = mark(iota((EDGES, EDGES), 0) < iota((EDGES, EDGES), 1))
    rank = jnp.sum(jnp.where(owned, dot(owned_b, before), 0.0), axis=0, keepdims=True)
    at_rank = rank.astype(I32) == iota((16, EDGES), 0)

    def table(values):
        return dot(owned_b, jnp.where(at_rank, values.astype(F32), 0.0).astype(BF16), NT)

    named = (table(jnp.ones((1, EDGES), I32)) - 1.0) * 8192.0
    srow, tid = srow_ref[...], tid_ref[...]
    want[...] = jnp.zeros_like(want)
    want[:, 0:16] = table(srow >> 4) * 16.0 + table(srow & 15) + named
    tgt_t[...] = table(tid >> 4) * 16.0 + table(tid & 15) + named
    rel_t[...] = table(rid_ref[...]) + named

    pl.semaphore_wait(barrier, NO - 1 + NI - 1)

    def send_i1(d, carry):
        po = outer_peer(d)
        remote(
            want.at[pl.ds(pl.multiple_of(po * NI, 8), NI)],
            r1.at[pl.ds(pl.multiple_of(o * NI, 8), NI)],
            i1s, i1r, po, i,
        ).start()
        return carry

    lax.fori_loop(1, NO, send_i1, 0)
    r1[pl.ds(pl.multiple_of(o * NI, 8), NI), :] = want[pl.ds(pl.multiple_of(o * NI, 8), NI), :]

    halves = (pl.ds(0, HALF), pl.ds(HALF, HALF))
    first = []
    for d in (1, 3, 2):
        for h, peer in enumerate((xp, zp)):
            cp = remote(
                pan_ref.at[halves[h]], pan_all.at[i, halves[h]],
                g1s.at[h, d - 1], g1r.at[h, d - 1], o, peer(d),
            )
            cp.start()
            first.append(cp)
    own_pan = pltpu.make_async_copy(pan_ref, pan_all.at[i], local_sem.at[1])
    own_pan.start()

    n1 = (NO - 1) * NI
    w1 = remote(want.at[pl.ds(0, n1)], r1.at[pl.ds(0, n1)], i1s, i1r, outer_peer(1), i)
    w1.wait_recv()
    for k in range(NI):
        s2[k * NO:(k + 1) * NO, :] = r1[pl.ds(k, NO, stride=NI), :]

    def send_i2(d, carry):
        pi = inner_peer(d)
        remote(
            s2.at[pl.ds(pl.multiple_of(pi * NO, 8), NO)],
            r2.at[pl.ds(pl.multiple_of(i * NO, 8), NO)],
            i2s, i2r, o, pi,
        ).start()
        return carry

    lax.fori_loop(1, NI, send_i2, 0)
    r2[pl.ds(pl.multiple_of(i * NO, 8), NO), :] = s2[pl.ds(pl.multiple_of(i * NO, 8), NO), :]
    second = []
    for d in (1, 3, 2):
        for h, peer in enumerate((zp, xp)):
            cp = remote(
                pan_ref.at[halves[h]], pan_all.at[i, halves[h]],
                g2s.at[h, 0, d - 1], g2r.at[h, 0, d - 1], o, peer(d),
            )
            cp.start()
            second.append(cp)

    load.wait()
    eh[D:DP, :] = jnp.zeros((DP - D, ROWS), BF16)
    el[D:DP, :] = jnp.zeros((DP - D, ROWS), BF16)

    def split_ent(j, carry):
        rows = pl.ds(pl.multiple_of(j * 16, 16), 16)
        hi, lo = split(entf[rows, :])
        eh[rows, :] = hi
        el[rows, :] = lo
        return carry

    lax.fori_loop(0, D // 16, split_ent, 0)

    n2 = (NI - 1) * NO
    w2 = remote(s2.at[pl.ds(0, n2)], r2.at[pl.ds(0, n2)], i2s, i2r, o, inner_peer(1))
    w2.wait_recv()

    for e in (1, 3, 2):
        for h in (0, 1):
            near, far = ((xp, zp), (zp, xp))[h]
            src = near(-e)
            remote(
                pan_ref.at[halves[h]], pan_all.at[src, halves[h]],
                g1s.at[h, e - 1], g1r.at[h, e - 1], o, src,
            ).wait_recv()
            for d in (1, 3, 2):
                cp = remote(
                    pan_all.at[src, halves[h]], pan_all.at[src, halves[h]],
                    g2s.at[h, e, d - 1], g2r.at[h, e, d - 1], o, far(d),
                )
                cp.start()
                second.append(cp)

    for j in range(3):
        for kk in range(4):
            k = 4 * j + kk
            ids = r2[:, k:k + 1].astype(I32)
            onehot[k * DEV:(k + 1) * DEV, :] = mark(ids == iota((DEV, ROWS), 1))
        rows = pl.ds(j * 4 * DEV, 4 * DEV)
        xs[rows, :] = dot(onehot[rows, :], eh[...], NT) + dot(onehot[rows, :], el[...], NT)

    def pack(src, dst):
        for k in range(CAP):
            for t in range(3):
                dst[pl.ds(3 * k + t, DEV, stride=MSG), :] = src[
                    k * DEV:(k + 1) * DEV, t * 128:(t + 1) * 128
                ]
        for half, ks in ((36, range(0, 8)), (37, range(8, CAP))):
            rest = None
            for k in ks:
                part = src[k * DEV:(k + 1) * DEV, 384:512]
                if k % 8:
                    part = pltpu.roll(part, 16 * (k % 8), 1)
                rest = part if rest is None else rest + part
            dst[pl.ds(half, DEV, stride=MSG), :] = rest

    def unpack(src, dst):
        tail = iota((DEV, 128), 1) < 16
        for k in range(CAP):
            for t in range(3):
                dst[k * DEV:(k + 1) * DEV, t * 128:(t + 1) * 128] = src[
                    pl.ds(3 * k + t, DEV, stride=MSG), :
                ]
            part = src[pl.ds(36 + k // 8, DEV, stride=MSG), :]
            if k % 8:
                part = pltpu.roll(part, 128 - 16 * (k % 8), 1)
            dst[k * DEV:(k + 1) * DEV, 384:512] = jnp.where(tail, part, 0.0)

    send_buf[pl.ds(38, DEV, stride=MSG), :] = jnp.zeros((DEV, 128), F32)
    send_buf[pl.ds(39, DEV, stride=MSG), :] = jnp.zeros((DEV, 128), F32)
    pack(xs, send_buf)

    def other(j):
        t, dc, b, a = j & 3, (j >> 2) & 1, (j >> 3) & 3, (j >> 5) & 3
        po = (((y + t + a) & 3) << 1) + ((c + dc) & 1)
        pi = (((z + t + b) & 3) << 2) + ((x + t) & 3)
        return po, pi

    def message(buf, n):
        return buf.at[pl.ds(pl.multiple_of(n * MSG, 8), MSG)]

    def send_rows(j, carry):
        po, pi = other(j)
        remote(message(send_buf, pi * NO + po), message(fetched, me), fs, fr, po, pi).start()
        return carry

    lax.fori_loop(1, DEV, send_rows, 0)
    own_rows = pltpu.make_async_copy(
        message(send_buf, mine), message(fetched, me), local_sem.at[2]
    )
    own_rows.start()

    neg = neg_ref[...]
    cnt[...] = dot(
        mark((neg >> 7) == iota((NI, EDGES), 0)), mark((neg & 127) == iota((PANEL, EDGES), 0)), NT
    )
    relh[...] = jnp.zeros_like(relh)
    rell[...] = jnp.zeros_like(rell)
    hi, lo = split(rel_ref[...])
    relh[0:D, 0:RELS] = hi
    rell[0:D, 0:RELS] = lo
    for k in range(CAP):
        rows = pl.ds(k * DEV, DEV)
        tcol[rows, :] = jnp.broadcast_to(tgt_t[:, k:k + 1], (DEV, 128)).astype(I32)
        rcol[rows, :] = jnp.broadcast_to(rel_t[:, k:k + 1], (DEV, 128)).astype(I32)
    ph[D:DP, :] = jnp.zeros((DP - D, ROWS), BF16)
    plo[D:DP, :] = jnp.zeros((DP - D, ROWS), BF16)
    relacc[...] = jnp.zeros_like(relacc)
    acc[...] = jnp.zeros_like(acc)

    own_pan.wait()
    for cp in first:
        cp.wait_send()
    for cp in second:
        cp.wait()
    for b in range(NI):
        hi, lo = split(pan_all[b])
        ph[0:D, b * PANEL:(b + 1) * PANEL] = hi
        plo[0:D, b * PANEL:(b + 1) * PANEL] = lo

    own_rows.wait()
    n3 = (DEV - 1) * MSG
    w3 = remote(send_buf.at[pl.ds(0, n3)], fetched.at[pl.ds(0, n3)], fs, fr, outer_peer(1), i)
    w3.wait_recv()
    w3.wait_send()
    w1.wait_send()
    w2.wait_send()
    unpack(fetched, xs)

    def block(j, carry):
        base = pl.multiple_of(j * BM, BM)
        rows = pl.ds(base, BM)
        rel_mark = mark(rcol[rows, 0:1] == iota((BM, 256), 1))
        rel_rows = dot(rel_mark, relh[...], NT) + dot(rel_mark, rell[...], NT)
        query = xs[rows, :] * rel_rows
        qh, ql = split(query)
        scores[...] = dot(qh, ph[...]) + dot(qh, plo[...]) + dot(ql, ph[...])

        def weigh(n, inner_carry):
            part = pl.ds(pl.multiple_of(n * 16, 16), 16)
            ids = tcol[pl.ds(pl.multiple_of(base + n * 16, 16), 16), :]
            total = jnp.zeros((16, 128), F32)
            picked = jnp.zeros((16, 128), F32)
            terms, hits = [], []
            for b in range(NI):
                s = scores[part, b * PANEL:(b + 1) * PANEL]
                hit = ids == iota((16, PANEL), 1) + b * PANEL
                e = jnp.exp(s) * cnt[b:b + 1, :]
                total += e
                picked += jnp.where(hit, s, 0.0)
                terms.append(e)
                hits.append(hit)
            z0 = jnp.sum(total, axis=1, keepdims=True)
            inv = 1.0 / (z0 + jnp.exp(jnp.sum(picked, axis=1, keepdims=True)))
            for b in range(NI):
                w = (terms[b] - jnp.where(hits[b], z0, 0.0)) * inv
                w_hi, w_lo = split(w)
                wh[part, b * PANEL:(b + 1) * PANEL] = w_hi
                wl[part, b * PANEL:(b + 1) * PANEL] = w_lo
            return inner_carry

        lax.fori_loop(0, BM // 16, weigh, 0)
        grad = dot(wh[...], ph[...], NT) + dot(wh[...], plo[...], NT) + dot(wl[...], ph[...], NT)
        gs[rows, :] = grad * rel_rows
        gh, gl = split((grad * xs[rows, :]).T[0:D])
        relacc[0:D, :] += dot(gh, rel_mark) + dot(gl, rel_mark)
        th, tl = split(query.T[0:D])
        for b in range(0, NI, 2):
            lanes = slice(b * PANEL, (b + 2) * PANEL)
            add = dot(th, wh[:, lanes]) + dot(th, wl[:, lanes]) + dot(tl, wh[:, lanes])
            acc[b // 4, b % 4] += add[:, 0:PANEL]
            acc[b // 4, b % 4 + 1] += add[:, PANEL:2 * PANEL]
        return carry

    lax.fori_loop(0, SLOTS // BM, block, 0)

    reduce1 = []
    for d in (1, 3, 2):
        cp = remote(
            acc.at[(z + d) & 3, :, halves[0]], rsa1.at[d - 1],
            p1s.at[0, d - 1], p1r.at[0, d - 1], o, zp(d),
        )
        cp.start()
        reduce1.append(cp)
        cp = remote(
            acc.at[:, (x + d) & 3, halves[1]], rsb1.at[d - 1],
            p1s.at[1, d - 1], p1r.at[1, d - 1], o, xp(d),
        )
        cp.start()
        reduce1.append(cp)

    def send_q1(d, carry):
        po = outer_peer(d)
        remote(
            relacc.at[pl.ds(pl.multiple_of(po * 64, 8), 64)], ra1.at[o], q1s, q1r, po, i
        ).start()
        return carry

    lax.fori_loop(1, NO, send_q1, 0)
    ra1[o] = relacc[pl.ds(pl.multiple_of(o * 64, 8), 64), :]

    pack(gs, send_buf)

    def send_grads(j, carry):
        po, pi = other(j)
        remote(
            message(send_buf, po * NI + pi), message(returned, mine), bs, br, po, pi
        ).start()
        return carry

    lax.fori_loop(1, DEV, send_grads, 0)
    own_grads = pltpu.make_async_copy(
        message(send_buf, me), message(returned, mine), local_sem.at[3]
    )
    own_grads.start()

    v1 = remote(ra1.at[pl.ds(0, NO - 1)], ra1.at[pl.ds(0, NO - 1)], q1s, q1r, outer_peer(1), i)
    v1.wait_recv()
    part = ra1[0]
    for n in range(1, NO):
        part = part + ra1[n]
    for n in range(NI):
        a1p[n] = part[8 * (n >> 1):8 * (n >> 1) + 8, 128 * (n & 1):128 * (n & 1) + 128]

    def send_q2(d, carry):
        pi = inner_peer(d)
        remote(a1p.at[pi], ra2.at[i], q2s, q2r, o, pi).start()
        return carry

    lax.fori_loop(1, NI, send_q2, 0)
    ra2[i] = a1p[i]

    for cp in reduce1:
        cp.wait()
    sa[...] = acc[z, :, 0:HALF] + rsa1[0] + rsa1[1] + rsa1[2]
    sb[...] = acc[:, x, HALF:D] + rsb1[0] + rsb1[1] + rsb1[2]
    reduce2 = []
    for d in (1, 3, 2):
        cp = remote(
            sa.at[(x + d) & 3], rsa2.at[d - 1], p2s.at[0, d - 1], p2r.at[0, d - 1], o, xp(d)
        )
        cp.start()
        reduce2.append(cp)
        cp = remote(
            sb.at[(z + d) & 3], rsb2.at[d - 1], p2s.at[1, d - 1], p2r.at[1, d - 1], o, zp(d)
        )
        cp.start()
        reduce2.append(cp)

    v2 = remote(a1p.at[pl.ds(0, NI - 1)], ra2.at[pl.ds(0, NI - 1)], q2s, q2r, o, inner_peer(1))
    v2.wait_recv()
    part = ra2[0]
    for n in range(1, NI):
        part = part + ra2[n]
    a3s[...] = part
    a3[i] = part

    def send_q3(d, carry):
        pi = inner_peer(d)
        remote(a3s, a3.at[i], q3s, q3r, o, pi).start()
        return carry

    lax.fori_loop(1, NI, send_q3, 0)
    v3 = remote(a1p.at[pl.ds(0, NI - 1)], a3.at[pl.ds(0, NI - 1)], q3s, q3r, o, inner_peer(1))
    v3.wait_recv()
    for n in range(NI):
        c4[o, 8 * (n >> 1):8 * (n >> 1) + 8, 128 * (n & 1):128 * (n & 1) + 128] = a3[n]

    def send_q4(d, carry):
        po = outer_peer(d)
        remote(c4.at[o], c4.at[o], q4s, q4r, po, i).start()
        return carry

    lax.fori_loop(1, NO, send_q4, 0)

    own_grads.wait()
    w4 = remote(send_buf.at[pl.ds(0, n3)], returned.at[pl.ds(0, n3)], bs, br, outer_peer(1), i)
    w4.wait_recv()
    unpack(returned, xs)
    for j in range(3):
        rows = pl.ds(j * DP, DP)
        th, tl = split(xs[rows, :].T[0:D])
        for b in range(0, NI, 4):
            lanes = slice(b * PANEL, (b + 4) * PANEL)
            add = dot(th, onehot[rows, lanes]) + dot(tl, onehot[rows, lanes])
            if j == 0:
                entf[:, lanes] = add
            else:
                entf[:, lanes] += add
    store = pltpu.make_async_copy(entf, eout_ref, local_sem.at[4])
    store.start()

    for cp in reduce2:
        cp.wait()
    pout_ref[0:HALF, :] = sa[x] + rsa2[0] + rsa2[1] + rsa2[2]
    pout_ref[HALF:D, :] = sb[z] + rsb2[0] + rsb2[1] + rsb2[2]

    v4 = remote(c4.at[pl.ds(0, NO - 1)], c4.at[pl.ds(0, NO - 1)], q4s, q4r, outer_peer(1), i)
    v4.wait_recv()
    for n in range(NO - 1):
        top = min(D, (n + 1) * 64)
        rout_ref[n * 64:top, :] = c4[n, 0:top - n * 64, 0:RELS]

    w4.wait_send()
    v1.wait_send()
    v2.wait_send()
    v3.wait_send()
    v4.wait_send()
    store.wait()


def on_device(
    entities, panel_rows, relations, source_owner, source_row, relation_ids, target_ids, negatives
):
    dma, vm = pltpu.SemaphoreType.DMA, pltpu.VMEM
    scratch = [
        vm((D, ROWS), F32), vm((DP, ROWS), BF16), vm((DP, ROWS), BF16),
        vm((DEV, 128), F32), vm((DEV, 16), F32), vm((DEV, 16), F32),
        vm((DEV, 128), F32), vm((DEV, 128), F32), vm((DEV, 128), F32),
        vm((NI, D, PANEL), F32), vm((DP, ROWS), BF16), vm((DP, ROWS), BF16),
        vm((DP, 256), BF16), vm((DP, 256), BF16), vm((NI, PANEL), F32),
        vm((DEV * MSG, 128), F32), vm((DEV * MSG, 128), F32), vm((DEV * MSG, 128), F32),
        vm((SLOTS, DP), F32), vm((SLOTS, DP), F32), vm((SLOTS, ROWS), BF16),
        vm((SLOTS, 128), I32), vm((SLOTS, 128), I32),
        vm((BM, ROWS), F32), vm((BM, ROWS), BF16), vm((BM, ROWS), BF16),
        vm((4, 4, D, PANEL), F32), vm((DP, 256), F32),
        vm((3, 4, HALF, PANEL), F32), vm((3, 4, HALF, PANEL), F32),
        vm((4, HALF, PANEL), F32), vm((4, HALF, PANEL), F32),
        vm((3, HALF, PANEL), F32), vm((3, HALF, PANEL), F32),
        vm((NO, 64, 256), F32), vm((NI, 8, 128), F32), vm((NI, 8, 128), F32),
        vm((8, 128), F32), vm((NI, 8, 128), F32), vm((NO, 64, 256), F32),
        dma((5,)), pltpu.SemaphoreType.REGULAR,
        dma, dma, dma, dma,
        dma((2, 3)), dma((2, 3)), dma((2, 4, 3)), dma((2, 4, 3)),
        dma, dma, dma, dma,
        dma((2, 3)), dma((2, 3)), dma((2, 3)), dma((2, 3)),
        dma, dma, dma, dma, dma, dma, dma, dma,
    ]
    vmem = pl.BlockSpec(memory_space=pltpu.VMEM)
    anyw = pl.BlockSpec(memory_space=pl.ANY)
    entity, panel, relation = pl.pallas_call(
        step_kernel,
        out_shape=(
            jax.ShapeDtypeStruct((D, ROWS), F32),
            jax.ShapeDtypeStruct((D, PANEL), F32),
            jax.ShapeDtypeStruct((D, RELS), F32),
        ),
        in_specs=[anyw] + [vmem] * 7,
        out_specs=(anyw, vmem, vmem),
        scratch_shapes=scratch,
        compiler_params=pltpu.CompilerParams(
            collective_id=0, has_side_effects=True, vmem_limit_bytes=61 * 2**20
        ),
        name="edge_step",
    )(
        entities.T, panel_rows.T, relations.T,
        source_owner.reshape(1, EDGES), source_row.reshape(1, EDGES),
        relation_ids.reshape(1, EDGES), target_ids.reshape(1, EDGES), negatives,
    )
    return entity.T, panel.T, relation.T


def solution(mesh):
    placed = (
        P(("outer", "inner"), None),
        P(("outer", "inner"), None),
        P(),
        P(("outer", "inner")),
        P(("outer", "inner")),
        P(("outer", "inner")),
        P(("outer", "inner")),
        P(("outer", "inner"), None),
    )
    return jax.shard_map(
        on_device,
        mesh=mesh,
        in_specs=placed,
        out_specs=(P(("outer", "inner"), None), P(("outer", "inner"), None), P()),
        check_vma=False,
    )
```

```python
import jax
import jax.numpy as jnp
from jax import lax
from jax.experimental import pallas as pl
from jax.experimental.pallas import tpu as pltpu
from jax.sharding import PartitionSpec as P

MESH = pl.DeviceIdType.MESH
F32, BF16, I32 = jnp.float32, jnp.bfloat16, jnp.int32

D, DP = 400, 512
HALF = 200
RELS = 240
ROWS = 2048
PANEL = 128
EDGES = 1024
CAP = 12
NO, NI = 8, 16
DEV = NO * NI
SLOTS = CAP * DEV
KH = CAP // 2
HALF_SLOTS = KH * DEV
MSG = 24
SENT = 19
BM = 256
BLOCKS = HALF_SLOTS // BM
KC = 1280

NN = (((1,), (0,)), ((), ()))
NT = (((1,), (1,)), ((), ()))


def dot(a, b, dims=NN):
    return lax.dot_general(a, b, dims, preferred_element_type=F32)


def split(x):
    hi = x.astype(BF16)
    return hi, (x - hi.astype(F32)).astype(BF16)


def iota(shape, dim):
    return lax.broadcasted_iota(I32, shape, dim)


def mark(cond):
    return jnp.where(cond, 1.0, 0.0).astype(BF16)


def step_kernel(
    ent_ref, pan_ref, rel_ref, owner_ref, srow_ref, rid_ref, tid_ref, neg_ref,
    eout_ref, pout_ref, rout_ref,
    entf, ecat, want, tgt_t, rel_t, r1, s2, r2,
    pan_all, pcat, relh, rell, cnt,
    send_buf, fetched, returned, xs, tcol, rcol,
    scores_a, scores_b, qcat, wh, wl, relacc,
    rsa1, rsb1, sa, sb, rsa2, rsb2,
    ra1, a1p, ra2, a3s, a3, c4,
    local_sem,
    i1s, i1r, i2s, i2r, g1s, g1r, g2s, g2r, fs, fr, bs, br,
    p1s, p1r, p2s, p2r, q1s, q1r, q2s, q2r, q3s, q3r, q4s, q4r,
):
    o, i = lax.axis_index("outer"), lax.axis_index("inner")
    me = o * NI + i
    mine = i * NO + o
    z, x = i >> 2, i & 3
    y, c = o >> 1, o & 1

    def outer_peer(d):
        return (o + d) & 7

    def inner_peer(d):
        return (i + d) & 15

    def xp(d):
        return (z << 2) + ((x + d) & 3)

    def zp(d):
        return (((z + d) & 3) << 2) + x

    def remote(src, dst, ss, rs, po, pi):
        return pltpu.make_async_remote_copy(
            src_ref=src, dst_ref=dst, send_sem=ss, recv_sem=rs,
            device_id=(po, pi), device_id_type=MESH,
        )

    barrier = pltpu.get_barrier_semaphore()

    def greet_outer(d, carry):
        pl.semaphore_signal(barrier, inc=1, device_id=(outer_peer(d), i), device_id_type=MESH)
        return carry

    def greet_inner(d, carry):
        pl.semaphore_signal(barrier, inc=1, device_id=(o, inner_peer(d)), device_id_type=MESH)
        return carry

    lax.fori_loop(1, NO, greet_outer, 0)
    lax.fori_loop(1, NI, greet_inner, 0)
    load = pltpu.make_async_copy(ent_ref, entf, local_sem.at[0])
    load.start()

    owner = owner_ref[...]
    owned = owner == iota((DEV, EDGES), 0)
    owned_b = mark(owned)
    before = mark(iota((EDGES, EDGES), 0) < iota((EDGES, EDGES), 1))
    rank = jnp.sum(jnp.where(owned, dot(owned_b, before), 0.0), axis=0, keepdims=True)
    at_rank = rank.astype(I32) == iota((16, EDGES), 0)

    def table(values):
        return dot(owned_b, jnp.where(at_rank, values.astype(F32), 0.0).astype(BF16), NT)

    named = (table(jnp.ones((1, EDGES), I32)) - 1.0) * 8192.0
    srow, tid = srow_ref[...], tid_ref[...]
    want[...] = jnp.zeros_like(want)
    want[:, 0:16] = table(srow >> 4) * 16.0 + table(srow & 15) + named
    tgt_t[...] = table(tid >> 4) * 16.0 + table(tid & 15) + named
    rel_t[...] = table(rid_ref[...]) + named

    pl.semaphore_wait(barrier, NO - 1 + NI - 1)

    def send_i1(d, carry):
        po = outer_peer(d)
        remote(
            want.at[pl.ds(pl.multiple_of(po * NI, 8), NI)],
            r1.at[pl.ds(pl.multiple_of(o * NI, 8), NI)],
            i1s, i1r, po, i,
        ).start()
        return carry

    lax.fori_loop(1, NO, send_i1, 0)
    r1[pl.ds(pl.multiple_of(o * NI, 8), NI), :] = want[pl.ds(pl.multiple_of(o * NI, 8), NI), :]

    halves = (pl.ds(0, HALF), pl.ds(HALF, HALF))
    first = []
    for d in (1, 3, 2):
        for h, peer in enumerate((xp, zp)):
            cp = remote(
                pan_ref.at[halves[h]], pan_all.at[z, x, halves[h]],
                g1s.at[h, d - 1], g1r.at[h, d - 1], o, peer(d),
            )
            cp.start()
            first.append(cp)
    own_pan = pltpu.make_async_copy(pan_ref, pan_all.at[z, x], local_sem.at[1])
    own_pan.start()

    n1 = (NO - 1) * NI
    w1 = remote(want.at[pl.ds(0, n1)], r1.at[pl.ds(0, n1)], i1s, i1r, outer_peer(1), i)
    w1.wait_recv()
    for k in range(NI):
        s2[k * NO:(k + 1) * NO, :] = r1[pl.ds(k, NO, stride=NI), :]

    def send_i2(d, carry):
        pi = inner_peer(d)
        remote(
            s2.at[pl.ds(pl.multiple_of(pi * NO, 8), NO)],
            r2.at[pl.ds(pl.multiple_of(i * NO, 8), NO)],
            i2s, i2r, o, pi,
        ).start()
        return carry

    lax.fori_loop(1, NI, send_i2, 0)
    r2[pl.ds(pl.multiple_of(i * NO, 8), NO), :] = s2[pl.ds(pl.multiple_of(i * NO, 8), NO), :]
    second = []
    for d in (1, 3, 2):
        for h, peer in enumerate((zp, xp)):
            cp = remote(
                pan_ref.at[halves[h]], pan_all.at[z, x, halves[h]],
                g2s.at[h, 0, d - 1], g2r.at[h, 0, d - 1], o, peer(d),
            )
            cp.start()
            second.append(cp)

    load.wait()
    ecat[D:DP, :] = jnp.zeros((DP - D, ROWS), BF16)
    ecat[DP + D:, :] = jnp.zeros((DP - D, ROWS), BF16)

    def split_ent(j, carry):
        rows = pl.ds(pl.multiple_of(j * 16, 16), 16)
        hi, lo = split(entf[rows, :])
        ecat[rows, :] = hi
        ecat[pl.ds(pl.multiple_of(DP + j * 16, 16), 16), :] = lo
        return carry

    lax.fori_loop(0, D // 16, split_ent, 0)

    n2 = (NI - 1) * NO
    w2 = remote(s2.at[pl.ds(0, n2)], r2.at[pl.ds(0, n2)], i2s, i2r, o, inner_peer(1))
    w2.wait_recv()

    for e in (1, 3, 2):
        for h in (0, 1):
            near, far = ((xp, zp), (zp, xp))[h]
            src = near(-e)
            remote(
                pan_ref.at[halves[h]], pan_all.at[src >> 2, src & 3, halves[h]],
                g1s.at[h, e - 1], g1r.at[h, e - 1], o, src,
            ).wait_recv()
            for d in (1, 3, 2):
                cp = remote(
                    pan_all.at[src >> 2, src & 3, halves[h]],
                    pan_all.at[src >> 2, src & 3, halves[h]],
                    g2s.at[h, e, d - 1], g2r.at[h, e, d - 1], o, far(d),
                )
                cp.start()
                second.append(cp)

    def mark_wanted(k, dst, at):
        ids = r2[:, k:k + 1].astype(I32)
        dst[at:at + DEV, :] = mark(ids == iota((DEV, ROWS), 1))

    def pack(h, dst):
        rest = None
        for kk in range(KH):
            at = h * HALF_SLOTS + kk * DEV
            for t in range(3):
                dst[h, pl.ds(3 * kk + t, DEV, stride=MSG), :] = xs[
                    at:at + DEV, t * 128:(t + 1) * 128
                ]
            part = xs[at:at + DEV, 384:512]
            if kk:
                part = pltpu.roll(part, 16 * kk, 1)
            rest = part if rest is None else rest + part
        dst[h, pl.ds(SENT - 1, DEV, stride=MSG), :] = rest

    def unpack(h, src):
        tail = iota((DEV, 128), 1) < 16
        rest = src[h, pl.ds(SENT - 1, DEV, stride=MSG), :]
        for kk in range(KH):
            at = h * HALF_SLOTS + kk * DEV
            for t in range(3):
                xs[at:at + DEV, t * 128:(t + 1) * 128] = src[
                    h, pl.ds(3 * kk + t, DEV, stride=MSG), :
                ]
            part = pltpu.roll(rest, 128 - 16 * kk, 1) if kk else rest
            xs[at:at + DEV, 384:512] = jnp.where(tail, part, 0.0)

    def other(j):
        t, dc, b, a = j & 3, (j >> 2) & 1, (j >> 3) & 3, (j >> 5) & 3
        po = (((y + t + a) & 3) << 1) + ((c + dc) & 1)
        pi = (((z + t + b) & 3) << 2) + ((x + t) & 3)
        return po, pi

    def message(buf, h, n):
        return buf.at[h, pl.ds(pl.multiple_of(n * MSG, 8), SENT)]

    sent = (DEV - 1) * SENT

    def all_messages(buf, h, ss, rs):
        part = buf.at[h, pl.ds(0, sent)]
        return remote(part, part, ss.at[h], rs.at[h], outer_peer(1), i)

    own = []
    for h in range(2):
        for kk in range(KH):
            mark_wanted(h * KH + kk, wh, kk * DEV)
        picks = wh[0:HALF_SLOTS, :]
        xs[h * HALF_SLOTS:(h + 1) * HALF_SLOTS, :] = dot(picks, ecat[0:DP], NT) + dot(
            picks, ecat[DP:], NT
        )
        pack(h, send_buf)

        def send_rows(j, carry, h=h):
            po, pi = other(j)
            remote(
                message(send_buf, h, pi * NO + po), message(fetched, h, me),
                fs.at[h], fr.at[h], po, pi,
            ).start()
            return carry

        lax.fori_loop(1, DEV, send_rows, 0)
        cp = pltpu.make_async_copy(
            message(send_buf, h, mine), message(fetched, h, me), local_sem.at[2 + h]
        )
        cp.start()
        own.append(cp)

    neg = neg_ref[...]
    cnt[...] = dot(
        mark((neg >> 7) == iota((NI, EDGES), 0)), mark((neg & 127) == iota((PANEL, EDGES), 0)), NT
    )
    relh[...] = jnp.zeros_like(relh)
    rell[...] = jnp.zeros_like(rell)
    hi, lo = split(rel_ref[...])
    relh[0:D, 0:RELS] = hi
    rell[0:D, 0:RELS] = lo
    for k in range(CAP):
        rows = pl.ds(k * DEV, DEV)
        tcol[rows, :] = jnp.broadcast_to(tgt_t[:, k:k + 1], (DEV, 128)).astype(I32)
        rcol[rows, :] = jnp.broadcast_to(rel_t[:, k:k + 1], (DEV, 128)).astype(I32)
    pcat[1200:KC, :] = jnp.zeros((KC - 1200, ROWS), BF16)
    relacc[...] = jnp.zeros_like(relacc)

    own_pan.wait()
    for cp in first:
        cp.wait_send()
    for cp in second:
        cp.wait()
    for b in range(NI):
        hi, lo = split(pan_all[b // 4, b % 4])
        lanes = slice(b * PANEL, (b + 1) * PANEL)
        pcat[0:384, lanes] = hi[0:384]
        pcat[384:768, lanes] = lo[0:384]
        pcat[768:1152, lanes] = hi[0:384]
        pcat[1152:1168, lanes] = hi[384:D]
        pcat[1168:1184, lanes] = lo[384:D]
        pcat[1184:1200, lanes] = hi[384:D]

    def rel_part(base):
        rel_mark = mark(rcol[pl.ds(base, BM), 0:1] == iota((BM, 256), 1))
        return rel_mark, dot(rel_mark, relh[...], NT) + dot(rel_mark, rell[...], NT)

    def queries(base):
        unused, rel_rows = rel_part(base)
        query = xs[base:base + BM, :] * rel_rows
        qh, ql = split(query)
        qcat[:, 0:384] = qh[:, 0:384]
        qcat[:, 384:768] = qh[:, 0:384]
        qcat[:, 768:1152] = ql[:, 0:384]
        last_h, last_l = qh[:, 384:512].astype(F32), ql[:, 384:512].astype(F32)
        last = last_h + pltpu.roll(last_h, 16, 1) + pltpu.roll(last_l, 32, 1)
        qcat[:, 1152:KC] = last.astype(BF16)
        th, tl = split(query.T[0:D])
        ecat[0:D, base:base + BM] = th
        ecat[D:2 * D, base:base + BM] = tl

    def score(dst, n):
        lanes = pl.ds(pl.multiple_of(n * 256, 256), 256)
        dst[:, lanes] = dot(qcat[...], pcat[:, lanes])

    def weigh(src, base, n):
        part = pl.ds(pl.multiple_of(n * 16, 16), 16)
        out = pl.ds(pl.multiple_of(base + n * 16, 16), 16)
        ids = tcol[out, :]
        total = jnp.zeros((16, 128), F32)
        picked = jnp.zeros((16, 128), F32)
        terms, hits = [], []
        for b in range(NI):
            s = src[part, b * PANEL:(b + 1) * PANEL]
            hit = ids == iota((16, PANEL), 1) + b * PANEL
            e = jnp.exp(s) * cnt[b:b + 1, :]
            total += e
            picked += jnp.where(hit, s, 0.0)
            terms.append(e)
            hits.append(hit)
        z0 = jnp.sum(total, axis=1, keepdims=True)
        inv = 1.0 / (z0 + jnp.exp(jnp.sum(picked, axis=1, keepdims=True)))
        for b in range(NI):
            w = (terms[b] - jnp.where(hits[b], z0, 0.0)) * inv
            w_hi, w_lo = split(w)
            wh[out, b * PANEL:(b + 1) * PANEL] = w_hi
            wl[out, b * PANEL:(b + 1) * PANEL] = w_lo

    def gradients(base):
        rows = slice(base, base + BM)
        rel_mark, rel_rows = rel_part(base)
        high = dot(wh[rows], pcat[0:768], NT)
        rest = dot(wh[rows], pcat[1152:KC], NT)
        low = dot(wl[rows], pcat[768:KC], NT)
        last = rest + pltpu.roll(rest, 112, 1) + low[:, 384:512]
        last = jnp.where(iota((BM, 128), 1) < 16, last, 0.0)
        main = high[:, 0:384] + high[:, 384:768] + low[:, 0:384]
        grad = jnp.concatenate([main, last], axis=1)
        gh, gl = split((grad * xs[rows, :]).T[0:D])
        both = dot(jnp.concatenate([gh, gl], axis=0), rel_mark)
        relacc[0:D, :] += both[0:D] + both[D:2 * D]
        xs[rows, :] = grad * rel_rows

    for h in range(2):
        own[h].wait()
        all_messages(fetched, h, fs, fr).wait_recv()
        unpack(h, fetched)
        buffers = (scores_a, scores_b)
        start = h * HALF_SLOTS
        queries(start)

        def first_scores(n, carry):
            score(scores_a, n)
            return carry

        lax.fori_loop(0, 8, first_scores, 0)
        for j in range(BLOCKS):
            base = start + j * BM
            now, later = buffers[j % 2], buffers[(j + 1) % 2]
            if j + 1 < BLOCKS:
                queries(base + BM)

            def weigh_and_score(n, carry, j=j, base=base, now=now, later=later):
                if j + 1 < BLOCKS:
                    score(later, n)
                weigh(now, base, 2 * n)
                weigh(now, base, 2 * n + 1)
                return carry

            lax.fori_loop(0, 8, weigh_and_score, 0)
            gradients(base)

        if h == 1:
            def send_q1(d, carry):
                po = outer_peer(d)
                remote(
                    relacc.at[pl.ds(pl.multiple_of(po * 64, 8), 64)], ra1.at[o], q1s, q1r, po, i
                ).start()
                return carry

            lax.fori_loop(1, NO, send_q1, 0)
            ra1[o] = relacc[pl.ds(pl.multiple_of(o * 64, 8), 64), :]

        all_messages(send_buf, h, fs, fr).wait_send()
        pack(h, send_buf)

        def send_grads(j, carry, h=h):
            po, pi = other(j)
            remote(
                message(send_buf, h, po * NI + pi), message(returned, h, mine),
                bs.at[h], br.at[h], po, pi,
            ).start()
            return carry

        lax.fori_loop(1, DEV, send_grads, 0)
        cp = pltpu.make_async_copy(
            message(send_buf, h, me), message(returned, h, mine), local_sem.at[4 + h]
        )
        cp.start()
        own.append(cp)

    w1.wait_send()
    w2.wait_send()

    reduce1a, reduce1b = [], []
    for d in (1, 3, 2, 0):
        zb = (z + d) & 3
        for pair in range(2):
            lanes = pl.ds(pl.multiple_of(zb * 512 + pair * 256, 256), 256)
            both = dot(ecat[0:2 * D, 0:SLOTS], wh[:, lanes])
            add = both[0:D] + both[D:2 * D] + dot(ecat[0:D, 0:SLOTS], wl[:, lanes])
            pan_all[zb, 2 * pair] = add[:, 0:PANEL]
            pan_all[zb, 2 * pair + 1] = add[:, PANEL:2 * PANEL]
        if d:
            cp = remote(
                pan_all.at[zb, :, halves[0]], rsa1.at[d - 1],
                p1s.at[0, d - 1], p1r.at[0, d - 1], o, zp(d),
            )
            cp.start()
            reduce1a.append(cp)
    for d in (1, 3, 2):
        cp = remote(
            pan_all.at[:, (x + d) & 3, halves[1]], rsb1.at[d - 1],
            p1s.at[1, d - 1], p1r.at[1, d - 1], o, xp(d),
        )
        cp.start()
        reduce1b.append(cp)

    v1 = remote(ra1.at[pl.ds(0, NO - 1)], ra1.at[pl.ds(0, NO - 1)], q1s, q1r, outer_peer(1), i)
    v1.wait_recv()
    part = ra1[0]
    for n in range(1, NO):
        part = part + ra1[n]
    for n in range(NI):
        a1p[n] = part[8 * (n >> 1):8 * (n >> 1) + 8, 128 * (n & 1):128 * (n & 1) + 128]

    def send_q2(d, carry):
        pi = inner_peer(d)
        remote(a1p.at[pi], ra2.at[i], q2s, q2r, o, pi).start()
        return carry

    lax.fori_loop(1, NI, send_q2, 0)
    ra2[i] = a1p[i]

    reduce2 = []
    for cp in reduce1a:
        cp.wait()
    sa[...] = pan_all[z, :, 0:HALF] + rsa1[0] + rsa1[1] + rsa1[2]
    for d in (1, 3, 2):
        cp = remote(
            sa.at[(x + d) & 3], rsa2.at[d - 1], p2s.at[0, d - 1], p2r.at[0, d - 1], o, xp(d)
        )
        cp.start()
        reduce2.append(cp)

    def add_rows(h):
        own[2 + h].wait()
        all_messages(returned, h, bs, br).wait_recv()
        unpack(h, returned)
        for kk in range(KH):
            mark_wanted(h * KH + kk, wh, h * HALF_SLOTS + kk * DEV)
        rows = slice(h * HALF_SLOTS, (h + 1) * HALF_SLOTS)
        both = jnp.concatenate(split(xs[rows, :].T[0:D]), axis=0)
        for b in range(0, NI, 2):
            lanes = slice(b * PANEL, (b + 2) * PANEL)
            add = dot(both, wh[rows, lanes])
            add = add[0:D] + add[D:2 * D]
            if h == 0:
                entf[:, lanes] = add
            else:
                entf[:, lanes] += add

    add_rows(0)

    v2 = remote(a1p.at[pl.ds(0, NI - 1)], ra2.at[pl.ds(0, NI - 1)], q2s, q2r, o, inner_peer(1))
    v2.wait_recv()
    part = ra2[0]
    for n in range(1, NI):
        part = part + ra2[n]
    a3s[...] = part
    a3[i] = part

    def send_q3(d, carry):
        pi = inner_peer(d)
        remote(a3s, a3.at[i], q3s, q3r, o, pi).start()
        return carry

    lax.fori_loop(1, NI, send_q3, 0)

    for cp in reduce1b:
        cp.wait()
    sb[...] = pan_all[:, x, HALF:D] + rsb1[0] + rsb1[1] + rsb1[2]
    for d in (1, 3, 2):
        cp = remote(
            sb.at[(z + d) & 3], rsb2.at[d - 1], p2s.at[1, d - 1], p2r.at[1, d - 1], o, zp(d)
        )
        cp.start()
        reduce2.append(cp)

    v3 = remote(a1p.at[pl.ds(0, NI - 1)], a3.at[pl.ds(0, NI - 1)], q3s, q3r, o, inner_peer(1))
    v3.wait_recv()
    for n in range(NI):
        c4[o, 8 * (n >> 1):8 * (n >> 1) + 8, 128 * (n & 1):128 * (n & 1) + 128] = a3[n]

    def send_q4(d, carry):
        po = outer_peer(d)
        remote(c4.at[o], c4.at[o], q4s, q4r, po, i).start()
        return carry

    lax.fori_loop(1, NO, send_q4, 0)

    add_rows(1)
    store = pltpu.make_async_copy(entf, eout_ref, local_sem.at[6])
    store.start()

    for cp in reduce2:
        cp.wait()
    pout_ref[0:HALF, :] = sa[x] + rsa2[0] + rsa2[1] + rsa2[2]
    pout_ref[HALF:D, :] = sb[z] + rsb2[0] + rsb2[1] + rsb2[2]

    v4 = remote(c4.at[pl.ds(0, NO - 1)], c4.at[pl.ds(0, NO - 1)], q4s, q4r, outer_peer(1), i)
    v4.wait_recv()
    for n in range(NO - 1):
        top = min(D, (n + 1) * 64)
        rout_ref[n * 64:top, :] = c4[n, 0:top - n * 64, 0:RELS]

    for h in range(2):
        all_messages(send_buf, h, bs, br).wait_send()
    for v in (v1, v2, v3, v4):
        v.wait_send()
    store.wait()


def on_device(
    entities, panel_rows, relations, source_owner, source_row, relation_ids, target_ids, negatives
):
    dma, vm = pltpu.SemaphoreType.DMA, pltpu.VMEM
    scratch = [
        vm((D, ROWS), F32), vm((2 * DP, ROWS), BF16),
        vm((DEV, 128), F32), vm((DEV, 16), F32), vm((DEV, 16), F32),
        vm((DEV, 128), F32), vm((DEV, 128), F32), vm((DEV, 128), F32),
        vm((4, 4, D, PANEL), F32), vm((KC, ROWS), BF16),
        vm((DP, 256), BF16), vm((DP, 256), BF16), vm((NI, PANEL), F32),
        vm((2, DEV * MSG, 128), F32), vm((2, DEV * MSG, 128), F32),
        vm((2, DEV * MSG, 128), F32), vm((SLOTS, DP), F32),
        vm((SLOTS, 128), I32), vm((SLOTS, 128), I32),
        vm((BM, ROWS), F32), vm((BM, ROWS), F32), vm((BM, KC), BF16),
        vm((SLOTS, ROWS), BF16), vm((SLOTS, ROWS), BF16), vm((DP, 256), F32),
        vm((3, 4, HALF, PANEL), F32), vm((3, 4, HALF, PANEL), F32),
        vm((4, HALF, PANEL), F32), vm((4, HALF, PANEL), F32),
        vm((3, HALF, PANEL), F32), vm((3, HALF, PANEL), F32),
        vm((NO, 64, 256), F32), vm((NI, 8, 128), F32), vm((NI, 8, 128), F32),
        vm((8, 128), F32), vm((NI, 8, 128), F32), vm((NO, 64, 256), F32),
        dma((7,)),
        dma, dma, dma, dma,
        dma((2, 3)), dma((2, 3)), dma((2, 4, 3)), dma((2, 4, 3)),
        dma((2,)), dma((2,)), dma((2,)), dma((2,)),
        dma((2, 3)), dma((2, 3)), dma((2, 3)), dma((2, 3)),
        dma, dma, dma, dma, dma, dma, dma, dma,
    ]
    vmem = pl.BlockSpec(memory_space=pltpu.VMEM)
    anyw = pl.BlockSpec(memory_space=pl.ANY)
    entity, panel, relation = pl.pallas_call(
        step_kernel,
        out_shape=(
            jax.ShapeDtypeStruct((D, ROWS), F32),
            jax.ShapeDtypeStruct((D, PANEL), F32),
            jax.ShapeDtypeStruct((D, RELS), F32),
        ),
        in_specs=[anyw] + [vmem] * 7,
        out_specs=(anyw, vmem, vmem),
        scratch_shapes=scratch,
        compiler_params=pltpu.CompilerParams(
            collective_id=0, has_side_effects=True, vmem_limit_bytes=61 * 2**20
        ),
        name="edge_step",
    )(
        entities.T, panel_rows.T, relations.T,
        source_owner.reshape(1, EDGES), source_row.reshape(1, EDGES),
        relation_ids.reshape(1, EDGES), target_ids.reshape(1, EDGES), negatives,
    )
    return entity.T, panel.T, relation.T


def solution(mesh):
    placed = (
        P(("outer", "inner"), None),
        P(("outer", "inner"), None),
        P(),
        P(("outer", "inner")),
        P(("outer", "inner")),
        P(("outer", "inner")),
        P(("outer", "inner")),
        P(("outer", "inner"), None),
    )
    return jax.shard_map(
        on_device,
        mesh=mesh,
        in_specs=placed,
        out_specs=(P(("outer", "inner"), None), P(("outer", "inner"), None), P()),
        check_vma=False,
    )
```

```python
import jax
import jax.numpy as jnp
from jax import lax
from jax.experimental import pallas as pl
from jax.experimental.pallas import tpu as pltpu
from jax.sharding import PartitionSpec as P

MESH = pl.DeviceIdType.MESH
F32, BF16, I32 = jnp.float32, jnp.bfloat16, jnp.int32

D, DP = 400, 512
HALF = 200
RELS = 240
ROWS = 2048
PANEL = 128
EDGES = 1024
CAP = 12
NO, NI = 8, 16
DEV = NO * NI
SLOTS = CAP * DEV
KH = CAP // 2
HALF_SLOTS = KH * DEV
MSG = 24
SENT = 19
BM = HALF_SLOTS
KC = 1280

NN = (((1,), (0,)), ((), ()))
NT = (((1,), (1,)), ((), ()))


def dot(a, b, dims=NN):
    return lax.dot_general(a, b, dims, preferred_element_type=F32)


def split(x):
    hi = x.astype(BF16)
    return hi, (x - hi.astype(F32)).astype(BF16)


def iota(shape, dim):
    return lax.broadcasted_iota(I32, shape, dim)


def mark(cond):
    return jnp.where(cond, 1.0, 0.0).astype(BF16)


def step_kernel(
    ent_ref, pan_ref, rel_ref, owner_ref, srow_ref, rid_ref, tid_ref, neg_ref,
    eout_ref, pout_ref, rout_ref,
    ecat, want, tgt_t, rel_t, r1, s2, r2,
    pan_all, pcat, relh, rell, cnt,
    send_buf, fetched, returned, xs, tcol, rcol,
    scores, qcat, wh, wl, relacc,
    rsa1, rsb1, sa, sb, rsa2, rsb2,
    ra1, a1p, ra2, a3s, a3, c4,
    local_sem,
    i1s, i1r, i2s, i2r, g1s, g1r, g2s, g2r, fs, fr, bs, br,
    p1s, p1r, p2s, p2r, q1s, q1r, q2s, q2r, q3s, q3r, q4s, q4r,
):
    o, i = lax.axis_index("outer"), lax.axis_index("inner")
    me = o * NI + i
    mine = i * NO + o
    z, x = i >> 2, i & 3
    y, c = o >> 1, o & 1

    def outer_peer(d):
        return (o + d) & 7

    def inner_peer(d):
        return (i + d) & 15

    def xp(d):
        return (z << 2) + ((x + d) & 3)

    def zp(d):
        return (((z + d) & 3) << 2) + x

    def remote(src, dst, ss, rs, po, pi):
        return pltpu.make_async_remote_copy(
            src_ref=src, dst_ref=dst, send_sem=ss, recv_sem=rs,
            device_id=(po, pi), device_id_type=MESH,
        )

    barrier = pltpu.get_barrier_semaphore()

    def greet_outer(d, carry):
        pl.semaphore_signal(barrier, inc=1, device_id=(outer_peer(d), i), device_id_type=MESH)
        return carry

    def greet_inner(d, carry):
        pl.semaphore_signal(barrier, inc=1, device_id=(o, inner_peer(d)), device_id_type=MESH)
        return carry

    lax.fori_loop(1, NO, greet_outer, 0)
    lax.fori_loop(1, NI, greet_inner, 0)
    entf = scores.at[pl.ds(0, D)]
    load = pltpu.make_async_copy(ent_ref, entf, local_sem.at[0])
    load.start()

    owner = owner_ref[...]
    owned = owner == iota((DEV, EDGES), 0)
    owned_b = mark(owned)
    before = mark(iota((EDGES, EDGES), 0) < iota((EDGES, EDGES), 1))
    rank = jnp.sum(jnp.where(owned, dot(owned_b, before), 0.0), axis=0, keepdims=True)
    at_rank = rank.astype(I32) == iota((16, EDGES), 0)

    def table(values):
        return dot(owned_b, jnp.where(at_rank, values.astype(F32), 0.0).astype(BF16), NT)

    named = (table(jnp.ones((1, EDGES), I32)) - 1.0) * 8192.0
    srow, tid = srow_ref[...], tid_ref[...]
    want[...] = jnp.zeros_like(want)
    want[:, 0:16] = table(srow >> 4) * 16.0 + table(srow & 15) + named
    tgt_t[...] = table(tid >> 4) * 16.0 + table(tid & 15) + named
    rel_t[...] = table(rid_ref[...]) + named

    pl.semaphore_wait(barrier, NO - 1 + NI - 1)

    def send_i1(d, carry):
        po = outer_peer(d)
        remote(
            want.at[pl.ds(pl.multiple_of(po * NI, 8), NI)],
            r1.at[pl.ds(pl.multiple_of(o * NI, 8), NI)],
            i1s, i1r, po, i,
        ).start()
        return carry

    lax.fori_loop(1, NO, send_i1, 0)
    r1[pl.ds(pl.multiple_of(o * NI, 8), NI), :] = want[pl.ds(pl.multiple_of(o * NI, 8), NI), :]

    halves = (pl.ds(0, HALF), pl.ds(HALF, HALF))
    first = []
    for d in (1, 3, 2):
        for h, peer in enumerate((xp, zp)):
            cp = remote(
                pan_ref.at[halves[h]], pan_all.at[z, x, halves[h]],
                g1s.at[h, d - 1], g1r.at[h, d - 1], o, peer(d),
            )
            cp.start()
            first.append(cp)
    own_pan = pltpu.make_async_copy(pan_ref, pan_all.at[z, x], local_sem.at[1])
    own_pan.start()

    n1 = (NO - 1) * NI
    w1 = remote(want.at[pl.ds(0, n1)], r1.at[pl.ds(0, n1)], i1s, i1r, outer_peer(1), i)
    w1.wait_recv()
    for k in range(NI):
        s2[k * NO:(k + 1) * NO, :] = r1[pl.ds(k, NO, stride=NI), :]

    def send_i2(d, carry):
        pi = inner_peer(d)
        remote(
            s2.at[pl.ds(pl.multiple_of(pi * NO, 8), NO)],
            r2.at[pl.ds(pl.multiple_of(i * NO, 8), NO)],
            i2s, i2r, o, pi,
        ).start()
        return carry

    lax.fori_loop(1, NI, send_i2, 0)
    r2[pl.ds(pl.multiple_of(i * NO, 8), NO), :] = s2[pl.ds(pl.multiple_of(i * NO, 8), NO), :]
    second = []
    for d in (1, 3, 2):
        for h, peer in enumerate((zp, xp)):
            cp = remote(
                pan_ref.at[halves[h]], pan_all.at[z, x, halves[h]],
                g2s.at[h, 0, d - 1], g2r.at[h, 0, d - 1], o, peer(d),
            )
            cp.start()
            second.append(cp)

    load.wait()
    ecat[D:DP, :] = jnp.zeros((DP - D, ROWS), BF16)
    ecat[DP + D:, :] = jnp.zeros((DP - D, ROWS), BF16)

    def split_ent(j, carry):
        rows = pl.ds(pl.multiple_of(j * 16, 16), 16)
        hi, lo = split(entf[rows, :])
        ecat[rows, :] = hi
        ecat[pl.ds(pl.multiple_of(DP + j * 16, 16), 16), :] = lo
        return carry

    lax.fori_loop(0, D // 16, split_ent, 0)

    n2 = (NI - 1) * NO
    w2 = remote(s2.at[pl.ds(0, n2)], r2.at[pl.ds(0, n2)], i2s, i2r, o, inner_peer(1))
    w2.wait_recv()

    for e in (1, 3, 2):
        for h in (0, 1):
            near, far = ((xp, zp), (zp, xp))[h]
            src = near(-e)
            remote(
                pan_ref.at[halves[h]], pan_all.at[src >> 2, src & 3, halves[h]],
                g1s.at[h, e - 1], g1r.at[h, e - 1], o, src,
            ).wait_recv()
            for d in (1, 3, 2):
                cp = remote(
                    pan_all.at[src >> 2, src & 3, halves[h]],
                    pan_all.at[src >> 2, src & 3, halves[h]],
                    g2s.at[h, e, d - 1], g2r.at[h, e, d - 1], o, far(d),
                )
                cp.start()
                second.append(cp)

    def mark_wanted(k, dst, at):
        ids = r2[:, k:k + 1].astype(I32)
        dst[at:at + DEV, :] = mark(ids == iota((DEV, ROWS), 1))

    def pack(h, dst):
        rest = None
        for kk in range(KH):
            at = h * HALF_SLOTS + kk * DEV
            for t in range(3):
                dst[h, pl.ds(3 * kk + t, DEV, stride=MSG), :] = xs[
                    at:at + DEV, t * 128:(t + 1) * 128
                ]
            part = xs[at:at + DEV, 384:512]
            if kk:
                part = pltpu.roll(part, 16 * kk, 1)
            rest = part if rest is None else rest + part
        dst[h, pl.ds(SENT - 1, DEV, stride=MSG), :] = rest

    def unpack(h, src):
        tail = iota((DEV, 128), 1) < 16
        rest = src[h, pl.ds(SENT - 1, DEV, stride=MSG), :]
        for kk in range(KH):
            at = h * HALF_SLOTS + kk * DEV
            for t in range(3):
                xs[at:at + DEV, t * 128:(t + 1) * 128] = src[
                    h, pl.ds(3 * kk + t, DEV, stride=MSG), :
                ]
            part = pltpu.roll(rest, 128 - 16 * kk, 1) if kk else rest
            xs[at:at + DEV, 384:512] = jnp.where(tail, part, 0.0)

    def other(j):
        t, dc, b, a = j & 3, (j >> 2) & 1, (j >> 3) & 3, (j >> 5) & 3
        po = (((y + t + a) & 3) << 1) + ((c + dc) & 1)
        pi = (((z + t + b) & 3) << 2) + ((x + t) & 3)
        return po, pi

    def message(buf, h, n):
        return buf.at[h, pl.ds(pl.multiple_of(n * MSG, 8), SENT)]

    sent = (DEV - 1) * SENT

    def all_messages(buf, h, ss, rs):
        part = buf.at[h, pl.ds(0, sent)]
        return remote(part, part, ss.at[h], rs.at[h], outer_peer(1), i)

    own = []
    for h in range(2):
        for kk in range(KH):
            mark_wanted(h * KH + kk, wh, kk * DEV)
        picks = wh[0:HALF_SLOTS, :]
        xs[h * HALF_SLOTS:(h + 1) * HALF_SLOTS, :] = dot(picks, ecat[0:DP], NT) + dot(
            picks, ecat[DP:], NT
        )
        pack(h, send_buf)

        def send_rows(j, carry, h=h):
            po, pi = other(j)
            remote(
                message(send_buf, h, pi * NO + po), message(fetched, h, me),
                fs.at[h], fr.at[h], po, pi,
            ).start()
            return carry

        lax.fori_loop(1, DEV, send_rows, 0)
        cp = pltpu.make_async_copy(
            message(send_buf, h, mine), message(fetched, h, me), local_sem.at[2 + h]
        )
        cp.start()
        own.append(cp)

    neg = neg_ref[...]
    cnt[...] = dot(
        mark((neg >> 7) == iota((NI, EDGES), 0)), mark((neg & 127) == iota((PANEL, EDGES), 0)), NT
    )
    relh[...] = jnp.zeros_like(relh)
    rell[...] = jnp.zeros_like(rell)
    hi, lo = split(rel_ref[...])
    relh[0:D, 0:RELS] = hi
    rell[0:D, 0:RELS] = lo
    for k in range(CAP):
        rows = pl.ds(k * DEV, DEV)
        tcol[rows, :] = jnp.broadcast_to(tgt_t[:, k:k + 1], (DEV, 128)).astype(I32)
        rcol[rows, :] = jnp.broadcast_to(rel_t[:, k:k + 1], (DEV, 128)).astype(I32)
    pcat[1200:KC, :] = jnp.zeros((KC - 1200, ROWS), BF16)
    relacc[...] = jnp.zeros_like(relacc)

    own_pan.wait()
    for cp in first:
        cp.wait_send()
    for cp in second:
        cp.wait()
    for b in range(NI):
        hi, lo = split(pan_all[b // 4, b % 4])
        lanes = slice(b * PANEL, (b + 1) * PANEL)
        pcat[0:384, lanes] = hi[0:384]
        pcat[384:768, lanes] = lo[0:384]
        pcat[768:1152, lanes] = hi[0:384]
        pcat[1152:1168, lanes] = hi[384:D]
        pcat[1168:1184, lanes] = lo[384:D]
        pcat[1184:1200, lanes] = hi[384:D]

    def rel_part(base):
        rel_mark = mark(rcol[pl.ds(base, BM), 0:1] == iota((BM, 256), 1))
        return rel_mark, dot(rel_mark, relh[...], NT) + dot(rel_mark, rell[...], NT)

    def queries(base):
        unused, rel_rows = rel_part(base)
        query = xs[base:base + BM, :] * rel_rows
        qh, ql = split(query)
        qcat[:, 0:384] = qh[:, 0:384]
        qcat[:, 384:768] = qh[:, 0:384]
        qcat[:, 768:1152] = ql[:, 0:384]
        last_h, last_l = qh[:, 384:512].astype(F32), ql[:, 384:512].astype(F32)
        last = last_h + pltpu.roll(last_h, 16, 1) + pltpu.roll(last_l, 32, 1)
        qcat[:, 1152:KC] = last.astype(BF16)
        th, tl = split(query.T[0:D])
        ecat[0:D, base:base + BM] = th
        ecat[D:2 * D, base:base + BM] = tl

    def weigh(n, base):
        part = pl.ds(pl.multiple_of(n * 16, 16), 16)
        out = pl.ds(pl.multiple_of(base + n * 16, 16), 16)
        ids = tcol[out, :] - iota((16, PANEL), 1)
        total = jnp.zeros((16, 128), F32)
        picked = jnp.zeros((16, 128), F32)
        terms = []
        for b in range(NI):
            s = scores[part, b * PANEL:(b + 1) * PANEL]
            e = jnp.exp(s) * cnt[b:b + 1, :]
            total += e
            picked = jnp.where(ids == b * PANEL, s, picked)
            terms.append(e)
        z0 = jnp.sum(total, axis=1, keepdims=True)
        inv = 1.0 / (z0 + jnp.exp(jnp.sum(picked, axis=1, keepdims=True)))
        taken = z0 * inv
        for b in range(NI):
            w = terms[b] * inv
            w = jnp.where(ids == b * PANEL, w - taken, w)
            w_hi, w_lo = split(w)
            wh[out, b * PANEL:(b + 1) * PANEL] = w_hi
            wl[out, b * PANEL:(b + 1) * PANEL] = w_lo

    def gradients(base):
        rows = slice(base, base + BM)
        rel_mark, rel_rows = rel_part(base)
        high = dot(wh[rows], pcat[0:768], NT)
        rest = dot(wh[rows], pcat[1152:KC], NT)
        low = dot(wl[rows], pcat[768:KC], NT)
        last = rest + pltpu.roll(rest, 112, 1) + low[:, 384:512]
        last = jnp.where(iota((BM, 128), 1) < 16, last, 0.0)
        main = high[:, 0:384] + high[:, 384:768] + low[:, 0:384]
        grad = jnp.concatenate([main, last], axis=1)
        gh, gl = split((grad * xs[rows, :]).T[0:D])
        both = dot(jnp.concatenate([gh, gl], axis=0), rel_mark)
        relacc[0:D, :] += both[0:D] + both[D:2 * D]
        xs[rows, :] = grad * rel_rows

    for h in range(2):
        own[h].wait()
        all_messages(fetched, h, fs, fr).wait_recv()
        unpack(h, fetched)
        start = h * HALF_SLOTS
        queries(start)
        scores[...] = dot(qcat[...], pcat[...])

        def weigh_rows(n, carry, start=start):
            weigh(n, start)
            return carry

        lax.fori_loop(0, BM // 16, weigh_rows, 0, unroll=4)
        gradients(start)

        if h == 1:
            def send_q1(d, carry):
                po = outer_peer(d)
                remote(
                    relacc.at[pl.ds(pl.multiple_of(po * 64, 8), 64)], ra1.at[o], q1s, q1r, po, i
                ).start()
                return carry

            lax.fori_loop(1, NO, send_q1, 0)
            ra1[o] = relacc[pl.ds(pl.multiple_of(o * 64, 8), 64), :]

        all_messages(send_buf, h, fs, fr).wait_send()
        pack(h, send_buf)

        def send_grads(j, carry, h=h):
            po, pi = other(j)
            remote(
                message(send_buf, h, po * NI + pi), message(returned, h, mine),
                bs.at[h], br.at[h], po, pi,
            ).start()
            return carry

        lax.fori_loop(1, DEV, send_grads, 0)
        cp = pltpu.make_async_copy(
            message(send_buf, h, me), message(returned, h, mine), local_sem.at[4 + h]
        )
        cp.start()
        own.append(cp)

    w1.wait_send()
    w2.wait_send()

    reduce1a, reduce1b = [], []
    for d in (1, 3, 2, 0):
        zb = (z + d) & 3
        for pair in range(2):
            lanes = pl.ds(pl.multiple_of(zb * 512 + pair * 256, 256), 256)
            both = dot(ecat[0:2 * D, 0:SLOTS], wh[:, lanes])
            add = both[0:D] + both[D:2 * D] + dot(ecat[0:D, 0:SLOTS], wl[:, lanes])
            pan_all[zb, 2 * pair] = add[:, 0:PANEL]
            pan_all[zb, 2 * pair + 1] = add[:, PANEL:2 * PANEL]
        if d:
            cp = remote(
                pan_all.at[zb, :, halves[0]], rsa1.at[d - 1],
                p1s.at[0, d - 1], p1r.at[0, d - 1], o, zp(d),
            )
            cp.start()
            reduce1a.append(cp)
    for d in (1, 3, 2):
        cp = remote(
            pan_all.at[:, (x + d) & 3, halves[1]], rsb1.at[d - 1],
            p1s.at[1, d - 1], p1r.at[1, d - 1], o, xp(d),
        )
        cp.start()
        reduce1b.append(cp)

    v1 = remote(ra1.at[pl.ds(0, NO - 1)], ra1.at[pl.ds(0, NO - 1)], q1s, q1r, outer_peer(1), i)
    v1.wait_recv()
    part = ra1[0]
    for n in range(1, NO):
        part = part + ra1[n]
    for n in range(NI):
        a1p[n] = part[8 * (n >> 1):8 * (n >> 1) + 8, 128 * (n & 1):128 * (n & 1) + 128]

    def send_q2(d, carry):
        pi = inner_peer(d)
        remote(a1p.at[pi], ra2.at[i], q2s, q2r, o, pi).start()
        return carry

    lax.fori_loop(1, NI, send_q2, 0)
    ra2[i] = a1p[i]

    reduce2 = []
    for cp in reduce1a:
        cp.wait()
    sa[...] = pan_all[z, :, 0:HALF] + rsa1[0] + rsa1[1] + rsa1[2]
    for d in (1, 3, 2):
        cp = remote(
            sa.at[(x + d) & 3], rsa2.at[d - 1], p2s.at[0, d - 1], p2r.at[0, d - 1], o, xp(d)
        )
        cp.start()
        reduce2.append(cp)

    def add_rows(h):
        own[2 + h].wait()
        all_messages(returned, h, bs, br).wait_recv()
        unpack(h, returned)
        for kk in range(KH):
            mark_wanted(h * KH + kk, wh, h * HALF_SLOTS + kk * DEV)
        rows = slice(h * HALF_SLOTS, (h + 1) * HALF_SLOTS)
        both = jnp.concatenate(split(xs[rows, :].T[0:D]), axis=0)
        for b in range(0, NI, 2):
            lanes = slice(b * PANEL, (b + 2) * PANEL)
            add = dot(both, wh[rows, lanes])
            add = add[0:D] + add[D:2 * D]
            if h == 0:
                entf[:, lanes] = add
            else:
                entf[:, lanes] += add

    add_rows(0)

    v2 = remote(a1p.at[pl.ds(0, NI - 1)], ra2.at[pl.ds(0, NI - 1)], q2s, q2r, o, inner_peer(1))
    v2.wait_recv()
    part = ra2[0]
    for n in range(1, NI):
        part = part + ra2[n]
    a3s[...] = part
    a3[i] = part

    def send_q3(d, carry):
        pi = inner_peer(d)
        remote(a3s, a3.at[i], q3s, q3r, o, pi).start()
        return carry

    lax.fori_loop(1, NI, send_q3, 0)

    for cp in reduce1b:
        cp.wait()
    sb[...] = pan_all[:, x, HALF:D] + rsb1[0] + rsb1[1] + rsb1[2]
    for d in (1, 3, 2):
        cp = remote(
            sb.at[(z + d) & 3], rsb2.at[d - 1], p2s.at[1, d - 1], p2r.at[1, d - 1], o, zp(d)
        )
        cp.start()
        reduce2.append(cp)

    v3 = remote(a1p.at[pl.ds(0, NI - 1)], a3.at[pl.ds(0, NI - 1)], q3s, q3r, o, inner_peer(1))
    v3.wait_recv()
    for n in range(NI):
        c4[o, 8 * (n >> 1):8 * (n >> 1) + 8, 128 * (n & 1):128 * (n & 1) + 128] = a3[n]

    def send_q4(d, carry):
        po = outer_peer(d)
        remote(c4.at[o], c4.at[o], q4s, q4r, po, i).start()
        return carry

    lax.fori_loop(1, NO, send_q4, 0)

    add_rows(1)
    store = pltpu.make_async_copy(entf, eout_ref, local_sem.at[6])
    store.start()

    for cp in reduce2:
        cp.wait()
    pout_ref[0:HALF, :] = sa[x] + rsa2[0] + rsa2[1] + rsa2[2]
    pout_ref[HALF:D, :] = sb[z] + rsb2[0] + rsb2[1] + rsb2[2]

    v4 = remote(c4.at[pl.ds(0, NO - 1)], c4.at[pl.ds(0, NO - 1)], q4s, q4r, outer_peer(1), i)
    v4.wait_recv()
    for n in range(NO - 1):
        top = min(D, (n + 1) * 64)
        rout_ref[n * 64:top, :] = c4[n, 0:top - n * 64, 0:RELS]

    for h in range(2):
        all_messages(send_buf, h, bs, br).wait_send()
    for v in (v1, v2, v3, v4):
        v.wait_send()
    store.wait()


def on_device(
    entities, panel_rows, relations, source_owner, source_row, relation_ids, target_ids, negatives
):
    dma, vm = pltpu.SemaphoreType.DMA, pltpu.VMEM
    scratch = [
        vm((2 * DP, ROWS), BF16),
        vm((DEV, 128), F32), vm((DEV, 16), F32), vm((DEV, 16), F32),
        vm((DEV, 128), F32), vm((DEV, 128), F32), vm((DEV, 128), F32),
        vm((4, 4, D, PANEL), F32), vm((KC, ROWS), BF16),
        vm((DP, 256), BF16), vm((DP, 256), BF16), vm((NI, PANEL), F32),
        vm((2, DEV * MSG, 128), F32), vm((2, DEV * MSG, 128), F32),
        vm((2, DEV * MSG, 128), F32), vm((SLOTS, DP), F32),
        vm((SLOTS, 128), I32), vm((SLOTS, 128), I32),
        vm((BM, ROWS), F32), vm((BM, KC), BF16),
        vm((SLOTS, ROWS), BF16), vm((SLOTS, ROWS), BF16), vm((DP, 256), F32),
        vm((3, 4, HALF, PANEL), F32), vm((3, 4, HALF, PANEL), F32),
        vm((4, HALF, PANEL), F32), vm((4, HALF, PANEL), F32),
        vm((3, HALF, PANEL), F32), vm((3, HALF, PANEL), F32),
        vm((NO, 64, 256), F32), vm((NI, 8, 128), F32), vm((NI, 8, 128), F32),
        vm((8, 128), F32), vm((NI, 8, 128), F32), vm((NO, 64, 256), F32),
        dma((7,)),
        dma, dma, dma, dma,
        dma((2, 3)), dma((2, 3)), dma((2, 4, 3)), dma((2, 4, 3)),
        dma((2,)), dma((2,)), dma((2,)), dma((2,)),
        dma((2, 3)), dma((2, 3)), dma((2, 3)), dma((2, 3)),
        dma, dma, dma, dma, dma, dma, dma, dma,
    ]
    vmem = pl.BlockSpec(memory_space=pltpu.VMEM)
    anyw = pl.BlockSpec(memory_space=pl.ANY)
    entity, panel, relation = pl.pallas_call(
        step_kernel,
        out_shape=(
            jax.ShapeDtypeStruct((D, ROWS), F32),
            jax.ShapeDtypeStruct((D, PANEL), F32),
            jax.ShapeDtypeStruct((D, RELS), F32),
        ),
        in_specs=[anyw] + [vmem] * 7,
        out_specs=(anyw, vmem, vmem),
        scratch_shapes=scratch,
        compiler_params=pltpu.CompilerParams(
            collective_id=0, has_side_effects=True, vmem_limit_bytes=61 * 2**20
        ),
        name="edge_step",
    )(
        entities.T, panel_rows.T, relations.T,
        source_owner.reshape(1, EDGES), source_row.reshape(1, EDGES),
        relation_ids.reshape(1, EDGES), target_ids.reshape(1, EDGES), negatives,
    )
    return entity.T, panel.T, relation.T


def solution(mesh):
    placed = (
        P(("outer", "inner"), None),
        P(("outer", "inner"), None),
        P(),
        P(("outer", "inner")),
        P(("outer", "inner")),
        P(("outer", "inner")),
        P(("outer", "inner")),
        P(("outer", "inner"), None),
    )
    return jax.shard_map(
        on_device,
        mesh=mesh,
        in_specs=placed,
        out_specs=(P(("outer", "inner"), None), P(("outer", "inner"), None), P()),
        check_vma=False,
    )
```

```python
import jax
import jax.numpy as jnp
from jax import lax
from jax.experimental import pallas as pl
from jax.experimental.pallas import tpu as pltpu
from jax.sharding import PartitionSpec as P

MESH = pl.DeviceIdType.MESH
F32, BF16, I32 = jnp.float32, jnp.bfloat16, jnp.int32

D, DP = 400, 512
HALF = 200
RELS = 240
ROWS = 2048
PANEL = 128
EDGES = 1024
CAP = 12
NO, NI = 8, 16
DEV = NO * NI
SLOTS = CAP * DEV
KS = (8, 4)
FIRST = (0, 8)
MSG = (32, 16)
SENT = (25, 13)
AT = (0, 32 * 128)
BM = 1024
KC = 1280

NN = (((1,), (0,)), ((), ()))
NT = (((1,), (1,)), ((), ()))


def dot(a, b, dims=NN):
    return lax.dot_general(a, b, dims, preferred_element_type=F32)


def split(x):
    hi = x.astype(BF16)
    return hi, (x - hi.astype(F32)).astype(BF16)


def iota(shape, dim):
    return lax.broadcasted_iota(I32, shape, dim)


def mark(cond):
    return jnp.where(cond, 1.0, 0.0).astype(BF16)


def step_kernel(
    ent_ref, pan_ref, rel_ref, owner_ref, srow_ref, rid_ref, tid_ref, neg_ref,
    eout_ref, pout_ref, rout_ref,
    ecat, want, tgt_t, rel_t, r1, s2, r2,
    pan_all, pcat, relh, rell, cnt,
    send_buf, fetched, returned, xs, codes,
    scores, qcat, wh, wl, relacc,
    rsa1, rsb1, sa, sb, rsa2, rsb2,
    ra1, a1p, ra2, a3s, a3, c4,
    local_sem,
    i1s, i1r, i2s, i2r, g1s, g1r, g2s, g2r, fs, fr, bs, br,
    p1s, p1r, p2s, p2r, q1s, q1r, q2s, q2r, q3s, q3r, q4s, q4r,
):
    o, i = lax.axis_index("outer"), lax.axis_index("inner")
    me = o * NI + i
    mine = i * NO + o
    z, x = i >> 2, i & 3
    y, c = o >> 1, o & 1

    def outer_peer(d):
        return (o + d) & 7

    def inner_peer(d):
        return (i + d) & 15

    def xp(d):
        return (z << 2) + ((x + d) & 3)

    def zp(d):
        return (((z + d) & 3) << 2) + x

    def remote(src, dst, ss, rs, po, pi):
        return pltpu.make_async_remote_copy(
            src_ref=src, dst_ref=dst, send_sem=ss, recv_sem=rs,
            device_id=(po, pi), device_id_type=MESH,
        )

    barrier = pltpu.get_barrier_semaphore()

    def greet_outer(d, carry):
        pl.semaphore_signal(barrier, inc=1, device_id=(outer_peer(d), i), device_id_type=MESH)
        return carry

    def greet_inner(d, carry):
        pl.semaphore_signal(barrier, inc=1, device_id=(o, inner_peer(d)), device_id_type=MESH)
        return carry

    lax.fori_loop(1, NO, greet_outer, 0)
    lax.fori_loop(1, NI, greet_inner, 0)
    entf = scores.at[pl.ds(0, D)]
    load = pltpu.make_async_copy(ent_ref, entf, local_sem.at[0])
    load.start()

    owner = owner_ref[...]
    owned = owner == iota((DEV, EDGES), 0)
    owned_b = mark(owned)
    before = mark(iota((EDGES, EDGES), 0) < iota((EDGES, EDGES), 1))
    rank = jnp.sum(jnp.where(owned, dot(owned_b, before), 0.0), axis=0, keepdims=True)
    at_rank = rank.astype(I32) == iota((16, EDGES), 0)

    def table(values):
        return dot(owned_b, jnp.where(at_rank, values.astype(F32), 0.0).astype(BF16), NT)

    named = (table(jnp.ones((1, EDGES), I32)) - 1.0) * 8192.0
    srow, tid = srow_ref[...], tid_ref[...]
    want[...] = jnp.zeros_like(want)
    want[:, 0:16] = table(srow >> 4) * 16.0 + table(srow & 15) + named
    tgt_t[...] = table(tid >> 4) * 16.0 + table(tid & 15) + named
    rel_t[...] = jnp.where(named < 0.0, 255.0, table(rid_ref[...]))

    pl.semaphore_wait(barrier, NO - 1 + NI - 1)

    def send_i1(d, carry):
        po = outer_peer(d)
        remote(
            want.at[pl.ds(pl.multiple_of(po * NI, 8), NI)],
            r1.at[pl.ds(pl.multiple_of(o * NI, 8), NI)],
            i1s, i1r, po, i,
        ).start()
        return carry

    lax.fori_loop(1, NO, send_i1, 0)
    r1[pl.ds(pl.multiple_of(o * NI, 8), NI), :] = want[pl.ds(pl.multiple_of(o * NI, 8), NI), :]

    halves = (pl.ds(0, HALF), pl.ds(HALF, HALF))
    first = []
    for d in (1, 3, 2):
        for h, peer in enumerate((xp, zp)):
            cp = remote(
                pan_ref.at[halves[h]], pan_all.at[z, x, halves[h]],
                g1s.at[h, d - 1], g1r.at[h, d - 1], o, peer(d),
            )
            cp.start()
            first.append(cp)
    own_pan = pltpu.make_async_copy(pan_ref, pan_all.at[z, x], local_sem.at[1])
    own_pan.start()

    n1 = (NO - 1) * NI
    w1 = remote(want.at[pl.ds(0, n1)], r1.at[pl.ds(0, n1)], i1s, i1r, outer_peer(1), i)
    w1.wait_recv()
    for k in range(NI):
        s2[k * NO:(k + 1) * NO, :] = r1[pl.ds(k, NO, stride=NI), :]

    def send_i2(d, carry):
        pi = inner_peer(d)
        remote(
            s2.at[pl.ds(pl.multiple_of(pi * NO, 8), NO)],
            r2.at[pl.ds(pl.multiple_of(i * NO, 8), NO)],
            i2s, i2r, o, pi,
        ).start()
        return carry

    lax.fori_loop(1, NI, send_i2, 0)
    r2[pl.ds(pl.multiple_of(i * NO, 8), NO), :] = s2[pl.ds(pl.multiple_of(i * NO, 8), NO), :]
    second = []
    for d in (1, 3, 2):
        for h, peer in enumerate((zp, xp)):
            cp = remote(
                pan_ref.at[halves[h]], pan_all.at[z, x, halves[h]],
                g2s.at[h, 0, d - 1], g2r.at[h, 0, d - 1], o, peer(d),
            )
            cp.start()
            second.append(cp)

    load.wait()
    ecat[D:DP, :] = jnp.zeros((DP - D, ROWS), BF16)
    ecat[DP + D:, :] = jnp.zeros((DP - D, ROWS), BF16)

    def split_ent(j, carry):
        rows = pl.ds(pl.multiple_of(j * 16, 16), 16)
        hi, lo = split(entf[rows, :])
        ecat[rows, :] = hi
        ecat[pl.ds(pl.multiple_of(DP + j * 16, 16), 16), :] = lo
        return carry

    lax.fori_loop(0, D // 16, split_ent, 0)

    n2 = (NI - 1) * NO
    w2 = remote(s2.at[pl.ds(0, n2)], r2.at[pl.ds(0, n2)], i2s, i2r, o, inner_peer(1))
    w2.wait_recv()

    for e in (1, 3, 2):
        for h in (0, 1):
            near, far = ((xp, zp), (zp, xp))[h]
            src = near(-e)
            remote(
                pan_ref.at[halves[h]], pan_all.at[src >> 2, src & 3, halves[h]],
                g1s.at[h, e - 1], g1r.at[h, e - 1], o, src,
            ).wait_recv()
            for d in (1, 3, 2):
                cp = remote(
                    pan_all.at[src >> 2, src & 3, halves[h]],
                    pan_all.at[src >> 2, src & 3, halves[h]],
                    g2s.at[h, e, d - 1], g2r.at[h, e, d - 1], o, far(d),
                )
                cp.start()
                second.append(cp)

    def mark_wanted(k, dst, at):
        ids = r2[:, k:k + 1].astype(I32)
        dst[at:at + DEV, :] = mark(ids == iota((DEV, ROWS), 1))

    def rows_of(h, n):
        return pl.ds(AT[h] + n, DEV, stride=MSG[h])

    def pack(h, dst):
        rest = None
        for kk in range(KS[h]):
            at = (FIRST[h] + kk) * DEV
            for t in range(3):
                dst[rows_of(h, 3 * kk + t), :] = xs[at:at + DEV, t * 128:(t + 1) * 128]
            part = xs[at:at + DEV, 384:512]
            if kk:
                part = pltpu.roll(part, 16 * kk, 1)
            rest = part if rest is None else rest + part
        dst[rows_of(h, SENT[h] - 1), :] = rest

    def unpack(h, src):
        tail = iota((DEV, 128), 1) < 16
        rest = src[rows_of(h, SENT[h] - 1), :]
        for kk in range(KS[h]):
            at = (FIRST[h] + kk) * DEV
            for t in range(3):
                xs[at:at + DEV, t * 128:(t + 1) * 128] = src[rows_of(h, 3 * kk + t), :]
            part = pltpu.roll(rest, 128 - 16 * kk, 1) if kk else rest
            xs[at:at + DEV, 384:512] = jnp.where(tail, part, 0.0)

    def other(j):
        t, dc, b, a = j & 3, (j >> 2) & 1, (j >> 3) & 3, (j >> 5) & 3
        po = (((y + t + a) & 3) << 1) + ((c + dc) & 1)
        pi = (((z + t + b) & 3) << 2) + ((x + t) & 3)
        return po, pi

    def message(buf, h, n):
        return buf.at[pl.ds(pl.multiple_of(AT[h] + n * MSG[h], 8), SENT[h])]

    def all_messages(buf, h, ss, rs):
        part = buf.at[pl.ds(AT[h], (DEV - 1) * SENT[h])]
        return remote(part, part, ss.at[h], rs.at[h], outer_peer(1), i)

    own = []
    for h in range(2):
        for kk in range(KS[h]):
            mark_wanted(FIRST[h] + kk, wh, kk * DEV)
        picks = wh[0:KS[h] * DEV, :]
        xs[FIRST[h] * DEV:(FIRST[h] + KS[h]) * DEV, :] = dot(picks, ecat[0:DP], NT) + dot(
            picks, ecat[DP:], NT
        )
        pack(h, send_buf)

        def send_rows(j, carry, h=h):
            po, pi = other(j)
            remote(
                message(send_buf, h, pi * NO + po), message(fetched, h, me),
                fs.at[h], fr.at[h], po, pi,
            ).start()
            return carry

        lax.fori_loop(1, DEV, send_rows, 0)
        cp = pltpu.make_async_copy(
            message(send_buf, h, mine), message(fetched, h, me), local_sem.at[2 + h]
        )
        cp.start()
        own.append(cp)

    neg = neg_ref[...]
    cnt[...] = dot(
        mark((neg >> 7) == iota((NI, EDGES), 0)), mark((neg & 127) == iota((PANEL, EDGES), 0)), NT
    )
    relh[...] = jnp.zeros_like(relh)
    rell[...] = jnp.zeros_like(rell)
    hi, lo = split(rel_ref[...])
    relh[0:D, 0:RELS] = hi
    rell[0:D, 0:RELS] = lo
    for k in range(CAP):
        rows = pl.ds(k * DEV, DEV)
        code = tgt_t[:, k:k + 1] * 256.0 + rel_t[:, k:k + 1]
        codes[rows, :] = jnp.broadcast_to(code, (DEV, 128)).astype(I32)
    pcat[1200:KC, :] = jnp.zeros((KC - 1200, ROWS), BF16)
    relacc[...] = jnp.zeros_like(relacc)

    own_pan.wait()
    for cp in first:
        cp.wait_send()
    for cp in second:
        cp.wait()
    for b in range(NI):
        hi, lo = split(pan_all[b // 4, b % 4])
        lanes = slice(b * PANEL, (b + 1) * PANEL)
        pcat[0:384, lanes] = hi[0:384]
        pcat[384:768, lanes] = lo[0:384]
        pcat[768:1152, lanes] = hi[0:384]
        pcat[1152:1168, lanes] = hi[384:D]
        pcat[1168:1184, lanes] = lo[384:D]
        pcat[1184:1200, lanes] = hi[384:D]

    def rel_part(rows, count):
        rel_mark = mark((codes[rows, 0:1] & 255) == iota((count, 256), 1))
        return rel_mark, dot(rel_mark, relh[...], NT) + dot(rel_mark, rell[...], NT)

    def queries(base, at, count):
        into = slice(at, at + count)
        unused, rel_rows = rel_part(slice(base, base + count), count)
        query = xs[base:base + count, :] * rel_rows
        qh, ql = split(query)
        qcat[into, 0:384] = qh[:, 0:384]
        qcat[into, 384:768] = qh[:, 0:384]
        qcat[into, 768:1152] = ql[:, 0:384]
        last_h, last_l = qh[:, 384:512].astype(F32), ql[:, 384:512].astype(F32)
        last = last_h + pltpu.roll(last_h, 16, 1) + pltpu.roll(last_l, 32, 1)
        qcat[into, 1152:KC] = last.astype(BF16)
        th, tl = split(query.T[0:D])
        ecat[0:D, base:base + count] = th
        ecat[D:2 * D, base:base + count] = tl

    def weigh(n, base):
        part = pl.ds(pl.multiple_of(n * 16, 16), 16)
        out = pl.ds(pl.multiple_of(base + n * 16, 16), 16)
        ids = (codes[out, :] >> 8) - iota((16, PANEL), 1)
        total = jnp.zeros((16, 128), F32)
        picked = jnp.zeros((16, 128), F32)
        terms = []
        for b in range(NI):
            s = scores[part, b * PANEL:(b + 1) * PANEL]
            e = jnp.exp(s) * cnt[b:b + 1, :]
            total += e
            picked = jnp.where(ids == b * PANEL, s, picked)
            terms.append(e)
        z0 = jnp.sum(total, axis=1, keepdims=True)
        inv = 1.0 / (z0 + jnp.exp(jnp.sum(picked, axis=1, keepdims=True)))
        taken = z0 * inv
        for b in range(NI):
            w = terms[b] * inv
            w = jnp.where(ids == b * PANEL, w - taken, w)
            w_hi, w_lo = split(w)
            wh[out, b * PANEL:(b + 1) * PANEL] = w_hi
            wl[out, b * PANEL:(b + 1) * PANEL] = w_lo

    def gradients(base, count):
        rows = slice(base, base + count)
        rel_mark, rel_rows = rel_part(rows, count)
        high = dot(wh[rows], pcat[0:768], NT)
        rest = dot(wh[rows], pcat[1152:KC], NT)
        low = dot(wl[rows], pcat[768:KC], NT)
        last = rest + pltpu.roll(rest, 112, 1) + low[:, 384:512]
        last = jnp.where(iota((count, 128), 1) < 16, last, 0.0)
        main = high[:, 0:384] + high[:, 384:768] + low[:, 0:384]
        grad = jnp.concatenate([main, last], axis=1)
        gh, gl = split((grad * xs[rows, :]).T[0:D])
        both = dot(jnp.concatenate([gh, gl], axis=0), rel_mark)
        relacc[0:D, :] += both[0:D] + both[D:2 * D]
        xs[rows, :] = grad * rel_rows

    for h in range(2):
        own[h].wait()
        all_messages(fetched, h, fs, fr).wait_recv()
        unpack(h, fetched)
        start, count = FIRST[h] * DEV, KS[h] * DEV
        for at in range(0, count, 512):
            queries(start + at, at, 512)
        scores[0:count, :] = dot(qcat[0:count, :], pcat[...])

        def weigh_rows(n, carry, start=start):
            weigh(n, start)
            return carry

        lax.fori_loop(0, count // 16, weigh_rows, 0, unroll=4)
        for at in range(0, count, 512):
            gradients(start + at, 512)

        if h == 1:
            def send_q1(d, carry):
                po = outer_peer(d)
                remote(
                    relacc.at[pl.ds(pl.multiple_of(po * 64, 8), 64)], ra1.at[o], q1s, q1r, po, i
                ).start()
                return carry

            lax.fori_loop(1, NO, send_q1, 0)
            ra1[o] = relacc[pl.ds(pl.multiple_of(o * 64, 8), 64), :]

        all_messages(send_buf, h, fs, fr).wait_send()
        pack(h, send_buf)

        def send_grads(j, carry, h=h):
            po, pi = other(j)
            remote(
                message(send_buf, h, po * NI + pi), message(returned, h, mine),
                bs.at[h], br.at[h], po, pi,
            ).start()
            return carry

        lax.fori_loop(1, DEV, send_grads, 0)
        cp = pltpu.make_async_copy(
            message(send_buf, h, me), message(returned, h, mine), local_sem.at[4 + h]
        )
        cp.start()
        own.append(cp)

    w1.wait_send()
    w2.wait_send()

    reduce1a, reduce1b = [], []
    for d in (1, 3, 2, 0):
        zb = (z + d) & 3
        for pair in range(2):
            lanes = pl.ds(pl.multiple_of(zb * 512 + pair * 256, 256), 256)
            both = dot(ecat[0:2 * D, 0:SLOTS], wh[:, lanes])
            add = both[0:D] + both[D:2 * D] + dot(ecat[0:D, 0:SLOTS], wl[:, lanes])
            pan_all[zb, 2 * pair] = add[:, 0:PANEL]
            pan_all[zb, 2 * pair + 1] = add[:, PANEL:2 * PANEL]
        if d:
            cp = remote(
                pan_all.at[zb, :, halves[0]], rsa1.at[d - 1],
                p1s.at[0, d - 1], p1r.at[0, d - 1], o, zp(d),
            )
            cp.start()
            reduce1a.append(cp)
    for d in (1, 3, 2):
        cp = remote(
            pan_all.at[:, (x + d) & 3, halves[1]], rsb1.at[d - 1],
            p1s.at[1, d - 1], p1r.at[1, d - 1], o, xp(d),
        )
        cp.start()
        reduce1b.append(cp)

    v1 = remote(ra1.at[pl.ds(0, NO - 1)], ra1.at[pl.ds(0, NO - 1)], q1s, q1r, outer_peer(1), i)
    v1.wait_recv()
    part = ra1[0]
    for n in range(1, NO):
        part = part + ra1[n]
    for n in range(NI):
        a1p[n] = part[8 * (n >> 1):8 * (n >> 1) + 8, 128 * (n & 1):128 * (n & 1) + 128]

    def send_q2(d, carry):
        pi = inner_peer(d)
        remote(a1p.at[pi], ra2.at[i], q2s, q2r, o, pi).start()
        return carry

    lax.fori_loop(1, NI, send_q2, 0)
    ra2[i] = a1p[i]

    reduce2 = []
    for cp in reduce1a:
        cp.wait()
    sa[...] = pan_all[z, :, 0:HALF] + rsa1[0] + rsa1[1] + rsa1[2]
    for d in (1, 3, 2):
        cp = remote(
            sa.at[(x + d) & 3], rsa2.at[d - 1], p2s.at[0, d - 1], p2r.at[0, d - 1], o, xp(d)
        )
        cp.start()
        reduce2.append(cp)

    stores = []

    def add_rows(h):
        own[2 + h].wait()
        all_messages(returned, h, bs, br).wait_recv()
        unpack(h, returned)
        for k in range(FIRST[h], FIRST[h] + KS[h]):
            mark_wanted(k, wh, k * DEV)
        rows = slice(FIRST[h] * DEV, (FIRST[h] + KS[h]) * DEV)
        both = jnp.concatenate(split(xs[rows, :].T[0:D]), axis=0)
        for b in range(0, NI, 2):
            lanes = slice(b * PANEL, (b + 2) * PANEL)
            add = dot(both, wh[rows, lanes])
            add = add[0:D] + add[D:2 * D]
            if h == 0:
                entf[:, lanes] = add
            else:
                entf[:, lanes] += add
                cp = pltpu.make_async_copy(
                    entf.at[:, lanes], eout_ref.at[:, lanes], local_sem.at[6 + b // 2]
                )
                cp.start()
                stores.append(cp)

    add_rows(0)

    v2 = remote(a1p.at[pl.ds(0, NI - 1)], ra2.at[pl.ds(0, NI - 1)], q2s, q2r, o, inner_peer(1))
    v2.wait_recv()
    part = ra2[0]
    for n in range(1, NI):
        part = part + ra2[n]
    a3s[...] = part
    a3[i] = part

    def send_q3(d, carry):
        pi = inner_peer(d)
        remote(a3s, a3.at[i], q3s, q3r, o, pi).start()
        return carry

    lax.fori_loop(1, NI, send_q3, 0)

    for cp in reduce1b:
        cp.wait()
    sb[...] = pan_all[:, x, HALF:D] + rsb1[0] + rsb1[1] + rsb1[2]
    for d in (1, 3, 2):
        cp = remote(
            sb.at[(z + d) & 3], rsb2.at[d - 1], p2s.at[1, d - 1], p2r.at[1, d - 1], o, zp(d)
        )
        cp.start()
        reduce2.append(cp)

    v3 = remote(a1p.at[pl.ds(0, NI - 1)], a3.at[pl.ds(0, NI - 1)], q3s, q3r, o, inner_peer(1))
    v3.wait_recv()
    for n in range(NI):
        c4[o, 8 * (n >> 1):8 * (n >> 1) + 8, 128 * (n & 1):128 * (n & 1) + 128] = a3[n]

    def send_q4(d, carry):
        po = outer_peer(d)
        remote(c4.at[o], c4.at[o], q4s, q4r, po, i).start()
        return carry

    lax.fori_loop(1, NO, send_q4, 0)

    add_rows(1)

    for cp in reduce2:
        cp.wait()
    pout_ref[0:HALF, :] = sa[x] + rsa2[0] + rsa2[1] + rsa2[2]
    pout_ref[HALF:D, :] = sb[z] + rsb2[0] + rsb2[1] + rsb2[2]

    v4 = remote(c4.at[pl.ds(0, NO - 1)], c4.at[pl.ds(0, NO - 1)], q4s, q4r, outer_peer(1), i)
    v4.wait_recv()
    for n in range(NO - 1):
        top = min(D, (n + 1) * 64)
        rout_ref[n * 64:top, :] = c4[n, 0:top - n * 64, 0:RELS]

    for h in range(2):
        all_messages(send_buf, h, bs, br).wait_send()
    for v in (v1, v2, v3, v4):
        v.wait_send()
    for cp in stores:
        cp.wait()


def on_device(
    entities, panel_rows, relations, source_owner, source_row, relation_ids, target_ids, negatives
):
    dma, vm = pltpu.SemaphoreType.DMA, pltpu.VMEM
    scratch = [
        vm((2 * DP, ROWS), BF16),
        vm((DEV, 128), F32), vm((DEV, 16), F32), vm((DEV, 16), F32),
        vm((DEV, 128), F32), vm((DEV, 128), F32), vm((DEV, 128), F32),
        vm((4, 4, D, PANEL), F32), vm((KC, ROWS), BF16),
        vm((DP, 256), BF16), vm((DP, 256), BF16), vm((NI, PANEL), F32),
        vm((DEV * 48, 128), F32), vm((DEV * 48, 128), F32),
        vm((DEV * 48, 128), F32), vm((SLOTS, DP), F32),
        vm((SLOTS, 128), I32),
        vm((BM, ROWS), F32), vm((BM, KC), BF16),
        vm((SLOTS, ROWS), BF16), vm((SLOTS, ROWS), BF16), vm((DP, 256), F32),
        vm((3, 4, HALF, PANEL), F32), vm((3, 4, HALF, PANEL), F32),
        vm((4, HALF, PANEL), F32), vm((4, HALF, PANEL), F32),
        vm((3, HALF, PANEL), F32), vm((3, HALF, PANEL), F32),
        vm((NO, 64, 256), F32), vm((NI, 8, 128), F32), vm((NI, 8, 128), F32),
        vm((8, 128), F32), vm((NI, 8, 128), F32), vm((NO, 64, 256), F32),
        dma((14,)),
        dma, dma, dma, dma,
        dma((2, 3)), dma((2, 3)), dma((2, 4, 3)), dma((2, 4, 3)),
        dma((2,)), dma((2,)), dma((2,)), dma((2,)),
        dma((2, 3)), dma((2, 3)), dma((2, 3)), dma((2, 3)),
        dma, dma, dma, dma, dma, dma, dma, dma,
    ]
    vmem = pl.BlockSpec(memory_space=pltpu.VMEM)
    anyw = pl.BlockSpec(memory_space=pl.ANY)
    entity, panel, relation = pl.pallas_call(
        step_kernel,
        out_shape=(
            jax.ShapeDtypeStruct((D, ROWS), F32),
            jax.ShapeDtypeStruct((D, PANEL), F32),
            jax.ShapeDtypeStruct((D, RELS), F32),
        ),
        in_specs=[anyw] + [vmem] * 7,
        out_specs=(anyw, vmem, vmem),
        scratch_shapes=scratch,
        compiler_params=pltpu.CompilerParams(
            collective_id=0, has_side_effects=True, vmem_limit_bytes=62 * 2**20
        ),
        name="edge_step",
    )(
        entities.T, panel_rows.T, relations.T,
        source_owner.reshape(1, EDGES), source_row.reshape(1, EDGES),
        relation_ids.reshape(1, EDGES), target_ids.reshape(1, EDGES), negatives,
    )
    return entity.T, panel.T, relation.T


def solution(mesh):
    placed = (
        P(("outer", "inner"), None),
        P(("outer", "inner"), None),
        P(),
        P(("outer", "inner")),
        P(("outer", "inner")),
        P(("outer", "inner")),
        P(("outer", "inner")),
        P(("outer", "inner"), None),
    )
    return jax.shard_map(
        on_device,
        mesh=mesh,
        in_specs=placed,
        out_specs=(P(("outer", "inner"), None), P(("outer", "inner"), None), P()),
        check_vma=False,
    )
```

```python
import jax
import jax.numpy as jnp
from jax import lax
from jax.experimental import pallas as pl
from jax.experimental.pallas import tpu as pltpu
from jax.sharding import PartitionSpec as P

MESH = pl.DeviceIdType.MESH
F32, BF16, I32 = jnp.float32, jnp.bfloat16, jnp.int32

D, DP = 400, 512
HALF = 200
RELS = 240
ROWS = 2048
PANEL = 128
EDGES = 1024
CAP = 12
NO, NI = 8, 16
DEV = NO * NI
SLOTS = CAP * DEV
KH = CAP // 2
HALF_SLOTS = KH * DEV
MSG = 24
SENT = 19
BM = HALF_SLOTS
KC = 1280

NN = (((1,), (0,)), ((), ()))
NT = (((1,), (1,)), ((), ()))


def dot(a, b, dims=NN):
    return lax.dot_general(a, b, dims, preferred_element_type=F32)


def split(x):
    hi = x.astype(BF16)
    return hi, (x - hi.astype(F32)).astype(BF16)


def iota(shape, dim):
    return lax.broadcasted_iota(I32, shape, dim)


def mark(cond):
    return jnp.where(cond, 1.0, 0.0).astype(BF16)


def step_kernel(
    ent_ref, pan_ref, rel_ref, owner_ref, srow_ref, rid_ref, tid_ref, neg_ref,
    eout_ref, pout_ref, rout_ref,
    ecat, want, tgt_t, rel_t, r1, s2, r2,
    pan_all, pcat, relh, rell, cnt,
    send_buf, fetched, returned, xs, tcol, rcol,
    scores, qcat, wh, wl, relacc,
    rsa1, rsb1, sa, sb, rsa2, rsb2,
    ra1, a1p, ra2, a3s, a3, c4,
    local_sem,
    i1s, i1r, i2s, i2r, g1s, g1r, g2s, g2r, fs, fr, bs, br,
    p1s, p1r, p2s, p2r, q1s, q1r, q2s, q2r, q3s, q3r, q4s, q4r,
):
    o, i = lax.axis_index("outer"), lax.axis_index("inner")
    me = o * NI + i
    mine = i * NO + o
    z, x = i >> 2, i & 3
    y, c = o >> 1, o & 1

    def outer_peer(d):
        return (o + d) & 7

    def inner_peer(d):
        return (i + d) & 15

    def xp(d):
        return (z << 2) + ((x + d) & 3)

    def zp(d):
        return (((z + d) & 3) << 2) + x

    def remote(src, dst, ss, rs, po, pi):
        return pltpu.make_async_remote_copy(
            src_ref=src, dst_ref=dst, send_sem=ss, recv_sem=rs,
            device_id=(po, pi), device_id_type=MESH,
        )

    barrier = pltpu.get_barrier_semaphore()

    def greet_outer(d, carry):
        pl.semaphore_signal(barrier, inc=1, device_id=(outer_peer(d), i), device_id_type=MESH)
        return carry

    def greet_inner(d, carry):
        pl.semaphore_signal(barrier, inc=1, device_id=(o, inner_peer(d)), device_id_type=MESH)
        return carry

    lax.fori_loop(1, NO, greet_outer, 0)
    lax.fori_loop(1, NI, greet_inner, 0)
    entf = scores.at[pl.ds(0, D)]
    load = pltpu.make_async_copy(ent_ref, entf, local_sem.at[0])
    load.start()

    owner = owner_ref[...]
    owned = owner == iota((DEV, EDGES), 0)
    owned_b = mark(owned)
    before = mark(iota((EDGES, EDGES), 0) < iota((EDGES, EDGES), 1))
    rank = jnp.sum(jnp.where(owned, dot(owned_b, before), 0.0), axis=0, keepdims=True)
    at_rank = rank.astype(I32) == iota((16, EDGES), 0)

    def table(values):
        return dot(owned_b, jnp.where(at_rank, values.astype(F32), 0.0).astype(BF16), NT)

    named = (table(jnp.ones((1, EDGES), I32)) - 1.0) * 8192.0
    srow, tid = srow_ref[...], tid_ref[...]
    want[...] = jnp.zeros_like(want)
    want[:, 0:16] = table(srow >> 4) * 16.0 + table(srow & 15) + named
    tgt_t[...] = table(tid >> 4) * 16.0 + table(tid & 15) + named
    rel_t[...] = table(rid_ref[...]) + named

    pl.semaphore_wait(barrier, NO - 1 + NI - 1)

    def send_i1(d, carry):
        po = outer_peer(d)
        remote(
            want.at[pl.ds(pl.multiple_of(po * NI, 8), NI)],
            r1.at[pl.ds(pl.multiple_of(o * NI, 8), NI)],
            i1s, i1r, po, i,
        ).start()
        return carry

    lax.fori_loop(1, NO, send_i1, 0)
    r1[pl.ds(pl.multiple_of(o * NI, 8), NI), :] = want[pl.ds(pl.multiple_of(o * NI, 8), NI), :]

    halves = (pl.ds(0, HALF), pl.ds(HALF, HALF))
    first = []
    for d in (1, 3, 2):
        for h, peer in enumerate((xp, zp)):
            cp = remote(
                pan_ref.at[halves[h]], pan_all.at[z, x, halves[h]],
                g1s.at[h, d - 1], g1r.at[h, d - 1], o, peer(d),
            )
            cp.start()
            first.append(cp)
    own_pan = pltpu.make_async_copy(pan_ref, pan_all.at[z, x], local_sem.at[1])
    own_pan.start()

    n1 = (NO - 1) * NI
    w1 = remote(want.at[pl.ds(0, n1)], r1.at[pl.ds(0, n1)], i1s, i1r, outer_peer(1), i)
    w1.wait_recv()
    for k in range(NI):
        s2[k * NO:(k + 1) * NO, :] = r1[pl.ds(k, NO, stride=NI), :]

    def send_i2(d, carry):
        pi = inner_peer(d)
        remote(
            s2.at[pl.ds(pl.multiple_of(pi * NO, 8), NO)],
            r2.at[pl.ds(pl.multiple_of(i * NO, 8), NO)],
            i2s, i2r, o, pi,
        ).start()
        return carry

    lax.fori_loop(1, NI, send_i2, 0)
    r2[pl.ds(pl.multiple_of(i * NO, 8), NO), :] = s2[pl.ds(pl.multiple_of(i * NO, 8), NO), :]
    second = []
    for d in (1, 3, 2):
        for h, peer in enumerate((zp, xp)):
            cp = remote(
                pan_ref.at[halves[h]], pan_all.at[z, x, halves[h]],
                g2s.at[h, 0, d - 1], g2r.at[h, 0, d - 1], o, peer(d),
            )
            cp.start()
            second.append(cp)

    load.wait()
    ecat[D:DP, :] = jnp.zeros((DP - D, ROWS), BF16)
    ecat[DP + D:, :] = jnp.zeros((DP - D, ROWS), BF16)

    def split_ent(j, carry):
        rows = pl.ds(pl.multiple_of(j * 16, 16), 16)
        hi, lo = split(entf[rows, :])
        ecat[rows, :] = hi
        ecat[pl.ds(pl.multiple_of(DP + j * 16, 16), 16), :] = lo
        return carry

    lax.fori_loop(0, D // 16, split_ent, 0)

    n2 = (NI - 1) * NO
    w2 = remote(s2.at[pl.ds(0, n2)], r2.at[pl.ds(0, n2)], i2s, i2r, o, inner_peer(1))
    w2.wait_recv()

    for e in (1, 3, 2):
        for h in (0, 1):
            near, far = ((xp, zp), (zp, xp))[h]
            src = near(-e)
            remote(
                pan_ref.at[halves[h]], pan_all.at[src >> 2, src & 3, halves[h]],
                g1s.at[h, e - 1], g1r.at[h, e - 1], o, src,
            ).wait_recv()
            for d in (1, 3, 2):
                cp = remote(
                    pan_all.at[src >> 2, src & 3, halves[h]],
                    pan_all.at[src >> 2, src & 3, halves[h]],
                    g2s.at[h, e, d - 1], g2r.at[h, e, d - 1], o, far(d),
                )
                cp.start()
                second.append(cp)

    def mark_wanted(k, dst, at):
        ids = r2[:, k:k + 1].astype(I32)
        dst[at:at + DEV, :] = mark(ids == iota((DEV, ROWS), 1))

    def pack(h, dst):
        rest = None
        for kk in range(KH):
            at = h * HALF_SLOTS + kk * DEV
            for t in range(3):
                dst[h, pl.ds(3 * kk + t, DEV, stride=MSG), :] = xs[
                    at:at + DEV, t * 128:(t + 1) * 128
                ]
            part = xs[at:at + DEV, 384:512]
            if kk:
                part = pltpu.roll(part, 16 * kk, 1)
            rest = part if rest is None else rest + part
        dst[h, pl.ds(SENT - 1, DEV, stride=MSG), :] = rest

    def unpack(h, src):
        tail = iota((DEV, 128), 1) < 16
        rest = src[h, pl.ds(SENT - 1, DEV, stride=MSG), :]
        for kk in range(KH):
            at = h * HALF_SLOTS + kk * DEV
            for t in range(3):
                xs[at:at + DEV, t * 128:(t + 1) * 128] = src[
                    h, pl.ds(3 * kk + t, DEV, stride=MSG), :
                ]
            part = pltpu.roll(rest, 128 - 16 * kk, 1) if kk else rest
            xs[at:at + DEV, 384:512] = jnp.where(tail, part, 0.0)

    def other(j):
        t, dc, b, a = j & 3, (j >> 2) & 1, (j >> 3) & 3, (j >> 5) & 3
        po = (((y + t + a) & 3) << 1) + ((c + dc) & 1)
        pi = (((z + t + b) & 3) << 2) + ((x + t) & 3)
        return po, pi

    def message(buf, h, n):
        return buf.at[h, pl.ds(pl.multiple_of(n * MSG, 8), SENT)]

    sent = (DEV - 1) * SENT

    def all_messages(buf, h, ss, rs):
        part = buf.at[h, pl.ds(0, sent)]
        return remote(part, part, ss.at[h], rs.at[h], outer_peer(1), i)

    own = []
    for h in range(2):
        for kk in range(KH):
            mark_wanted(h * KH + kk, wh, kk * DEV)
        picks = wh[0:HALF_SLOTS, :]
        xs[h * HALF_SLOTS:(h + 1) * HALF_SLOTS, :] = dot(picks, ecat[0:DP], NT) + dot(
            picks, ecat[DP:], NT
        )
        pack(h, send_buf)

        def send_rows(j, carry, h=h):
            po, pi = other(j)
            remote(
                message(send_buf, h, pi * NO + po), message(fetched, h, me),
                fs.at[h], fr.at[h], po, pi,
            ).start()
            return carry

        lax.fori_loop(1, DEV, send_rows, 0)
        cp = pltpu.make_async_copy(
            message(send_buf, h, mine), message(fetched, h, me), local_sem.at[2 + h]
        )
        cp.start()
        own.append(cp)

    neg = neg_ref[...]
    cnt[...] = dot(
        mark((neg >> 7) == iota((NI, EDGES), 0)), mark((neg & 127) == iota((PANEL, EDGES), 0)), NT
    )
    relh[...] = jnp.zeros_like(relh)
    rell[...] = jnp.zeros_like(rell)
    hi, lo = split(rel_ref[...])
    relh[0:D, 0:RELS] = hi
    rell[0:D, 0:RELS] = lo
    for k in range(CAP):
        rows = pl.ds(k * DEV, DEV)
        tcol[rows, :] = jnp.broadcast_to(tgt_t[:, k:k + 1], (DEV, 128)).astype(I32)
        rcol[rows, :] = jnp.broadcast_to(rel_t[:, k:k + 1], (DEV, 128)).astype(I32)
    pcat[1200:KC, :] = jnp.zeros((KC - 1200, ROWS), BF16)
    relacc[...] = jnp.zeros_like(relacc)

    own_pan.wait()
    for cp in first:
        cp.wait_send()
    for cp in second:
        cp.wait()
    for b in range(NI):
        hi, lo = split(pan_all[b // 4, b % 4])
        lanes = slice(b * PANEL, (b + 1) * PANEL)
        pcat[0:384, lanes] = hi[0:384]
        pcat[384:768, lanes] = lo[0:384]
        pcat[768:1152, lanes] = hi[0:384]
        pcat[1152:1168, lanes] = hi[384:D]
        pcat[1168:1184, lanes] = lo[384:D]
        pcat[1184:1200, lanes] = hi[384:D]

    def rel_part(base):
        rel_mark = mark(rcol[pl.ds(base, BM), 0:1] == iota((BM, 256), 1))
        return rel_mark, dot(rel_mark, relh[...], NT) + dot(rel_mark, rell[...], NT)

    def queries(base):
        unused, rel_rows = rel_part(base)
        query = xs[base:base + BM, :] * rel_rows
        qh, ql = split(query)
        qcat[:, 0:384] = qh[:, 0:384]
        qcat[:, 384:768] = qh[:, 0:384]
        qcat[:, 768:1152] = ql[:, 0:384]
        last_h, last_l = qh[:, 384:512].astype(F32), ql[:, 384:512].astype(F32)
        last = last_h + pltpu.roll(last_h, 16, 1) + pltpu.roll(last_l, 32, 1)
        qcat[:, 1152:KC] = last.astype(BF16)
        th, tl = split(query.T[0:D])
        ecat[0:D, base:base + BM] = th
        ecat[D:2 * D, base:base + BM] = tl

    def weigh(n, base):
        part = pl.ds(pl.multiple_of(n * 16, 16), 16)
        out = pl.ds(pl.multiple_of(base + n * 16, 16), 16)
        ids = tcol[out, :] - iota((16, PANEL), 1)
        total = jnp.zeros((16, 128), F32)
        picked = jnp.zeros((16, 128), F32)
        terms = []
        for b in range(NI):
            s = scores[part, b * PANEL:(b + 1) * PANEL]
            e = jnp.exp(s) * cnt[b:b + 1, :]
            total += e
            picked = jnp.where(ids == b * PANEL, s, picked)
            terms.append(e)
        z0 = jnp.sum(total, axis=1, keepdims=True)
        inv = 1.0 / (z0 + jnp.exp(jnp.sum(picked, axis=1, keepdims=True)))
        taken = z0 * inv
        for b in range(NI):
            w = terms[b] * inv
            w = jnp.where(ids == b * PANEL, w - taken, w)
            w_hi, w_lo = split(w)
            wh[out, b * PANEL:(b + 1) * PANEL] = w_hi
            wl[out, b * PANEL:(b + 1) * PANEL] = w_lo

    def gradients(base):
        rows = slice(base, base + BM)
        rel_mark, rel_rows = rel_part(base)
        high = dot(wh[rows], pcat[0:768], NT)
        rest = dot(wh[rows], pcat[1152:KC], NT)
        low = dot(wl[rows], pcat[768:KC], NT)
        last = rest + pltpu.roll(rest, 112, 1) + low[:, 384:512]
        last = jnp.where(iota((BM, 128), 1) < 16, last, 0.0)
        main = high[:, 0:384] + high[:, 384:768] + low[:, 0:384]
        grad = jnp.concatenate([main, last], axis=1)
        gh, gl = split((grad * xs[rows, :]).T[0:D])
        both = dot(jnp.concatenate([gh, gl], axis=0), rel_mark)
        relacc[0:D, :] += both[0:D] + both[D:2 * D]
        xs[rows, :] = grad * rel_rows

    for h in range(2):
        own[h].wait()
        all_messages(fetched, h, fs, fr).wait_recv()
        unpack(h, fetched)
        start = h * HALF_SLOTS
        queries(start)
        scores[...] = dot(qcat[...], pcat[...])

        def weigh_rows(n, carry, start=start):
            weigh(n, start)
            return carry

        lax.fori_loop(0, BM // 16, weigh_rows, 0, unroll=4)
        gradients(start)

        if h == 1:
            def send_q1(d, carry):
                po = outer_peer(d)
                remote(
                    relacc.at[pl.ds(pl.multiple_of(po * 64, 8), 64)], ra1.at[o], q1s, q1r, po, i
                ).start()
                return carry

            lax.fori_loop(1, NO, send_q1, 0)
            ra1[o] = relacc[pl.ds(pl.multiple_of(o * 64, 8), 64), :]

        all_messages(send_buf, h, fs, fr).wait_send()
        pack(h, send_buf)

        def send_grads(j, carry, h=h):
            po, pi = other(j)
            remote(
                message(send_buf, h, po * NI + pi), message(returned, h, mine),
                bs.at[h], br.at[h], po, pi,
            ).start()
            return carry

        lax.fori_loop(1, DEV, send_grads, 0)
        cp = pltpu.make_async_copy(
            message(send_buf, h, me), message(returned, h, mine), local_sem.at[4 + h]
        )
        cp.start()
        own.append(cp)

    w1.wait_send()
    w2.wait_send()

    reduce1a, reduce1b = [], []
    def panel_pair(zb, pair):
        lanes = pl.ds(pl.multiple_of(zb * 512 + pair * 256, 256), 256)
        both = dot(ecat[0:2 * D, 0:SLOTS], wh[:, lanes])
        add = both[0:D] + both[D:2 * D] + dot(ecat[0:D, 0:SLOTS], wl[:, lanes])
        pan_all[zb, 2 * pair] = add[:, 0:PANEL]
        pan_all[zb, 2 * pair + 1] = add[:, PANEL:2 * PANEL]

    def send_column(xb):
        d = (xb - x) & 3
        cp = remote(
            pan_all.at[:, xb, halves[1]], rsb1.at[d - 1],
            p1s.at[1, d - 1], p1r.at[1, d - 1], o, (z << 2) + xb,
        )
        cp.start()
        reduce1b.append(cp)

    far = 1 - (x >> 1)
    for d in (1, 3, 2, 0):
        panel_pair((z + d) & 3, far)
    send_column(2 * far)
    send_column(2 * far + 1)
    for d in (1, 3, 2, 0):
        zb = (z + d) & 3
        panel_pair(zb, 1 - far)
        if d:
            cp = remote(
                pan_all.at[zb, :, halves[0]], rsa1.at[d - 1],
                p1s.at[0, d - 1], p1r.at[0, d - 1], o, zp(d),
            )
            cp.start()
            reduce1a.append(cp)
    send_column(x ^ 1)

    v1 = remote(ra1.at[pl.ds(0, NO - 1)], ra1.at[pl.ds(0, NO - 1)], q1s, q1r, outer_peer(1), i)
    v1.wait_recv()
    part = ra1[0]
    for n in range(1, NO):
        part = part + ra1[n]
    for n in range(NI):
        a1p[n] = part[8 * (n >> 1):8 * (n >> 1) + 8, 128 * (n & 1):128 * (n & 1) + 128]

    def send_q2(d, carry):
        pi = inner_peer(d)
        remote(a1p.at[pi], ra2.at[i], q2s, q2r, o, pi).start()
        return carry

    lax.fori_loop(1, NI, send_q2, 0)
    ra2[i] = a1p[i]

    reduce2 = []
    for cp in reduce1a:
        cp.wait()
    sa[...] = pan_all[z, :, 0:HALF] + rsa1[0] + rsa1[1] + rsa1[2]
    for d in (1, 3, 2):
        cp = remote(
            sa.at[(x + d) & 3], rsa2.at[d - 1], p2s.at[0, d - 1], p2r.at[0, d - 1], o, xp(d)
        )
        cp.start()
        reduce2.append(cp)

    stores = []

    def add_rows(h):
        own[2 + h].wait()
        all_messages(returned, h, bs, br).wait_recv()
        unpack(h, returned)
        for kk in range(KH):
            mark_wanted(h * KH + kk, wh, h * HALF_SLOTS + kk * DEV)
        rows = slice(h * HALF_SLOTS, (h + 1) * HALF_SLOTS)
        both = jnp.concatenate(split(xs[rows, :].T[0:D]), axis=0)
        for b in range(0, NI, 2):
            lanes = slice(b * PANEL, (b + 2) * PANEL)
            add = dot(both, wh[rows, lanes])
            add = add[0:D] + add[D:2 * D]
            if h == 0:
                entf[:, lanes] = add
            else:
                entf[:, lanes] += add
                cp = pltpu.make_async_copy(
                    entf.at[:, lanes], eout_ref.at[:, lanes], local_sem.at[6 + b // 2]
                )
                cp.start()
                stores.append(cp)

    add_rows(0)

    v2 = remote(a1p.at[pl.ds(0, NI - 1)], ra2.at[pl.ds(0, NI - 1)], q2s, q2r, o, inner_peer(1))
    v2.wait_recv()
    part = ra2[0]
    for n in range(1, NI):
        part = part + ra2[n]
    a3s[...] = part
    a3[i] = part

    def send_q3(d, carry):
        pi = inner_peer(d)
        remote(a3s, a3.at[i], q3s, q3r, o, pi).start()
        return carry

    lax.fori_loop(1, NI, send_q3, 0)

    for cp in reduce1b:
        cp.wait()
    sb[...] = pan_all[:, x, HALF:D] + rsb1[0] + rsb1[1] + rsb1[2]
    for d in (1, 3, 2):
        cp = remote(
            sb.at[(z + d) & 3], rsb2.at[d - 1], p2s.at[1, d - 1], p2r.at[1, d - 1], o, zp(d)
        )
        cp.start()
        reduce2.append(cp)

    v3 = remote(a1p.at[pl.ds(0, NI - 1)], a3.at[pl.ds(0, NI - 1)], q3s, q3r, o, inner_peer(1))
    v3.wait_recv()
    for n in range(NI):
        c4[o, 8 * (n >> 1):8 * (n >> 1) + 8, 128 * (n & 1):128 * (n & 1) + 128] = a3[n]

    def send_q4(d, carry):
        po = outer_peer(d)
        remote(c4.at[o], c4.at[o], q4s, q4r, po, i).start()
        return carry

    lax.fori_loop(1, NO, send_q4, 0)

    add_rows(1)

    for cp in reduce2:
        cp.wait()
    pout_ref[0:HALF, :] = sa[x] + rsa2[0] + rsa2[1] + rsa2[2]
    pout_ref[HALF:D, :] = sb[z] + rsb2[0] + rsb2[1] + rsb2[2]

    v4 = remote(c4.at[pl.ds(0, NO - 1)], c4.at[pl.ds(0, NO - 1)], q4s, q4r, outer_peer(1), i)
    v4.wait_recv()
    for n in range(NO - 1):
        top = min(D, (n + 1) * 64)
        rout_ref[n * 64:top, :] = c4[n, 0:top - n * 64, 0:RELS]

    for h in range(2):
        all_messages(send_buf, h, bs, br).wait_send()
    for v in (v1, v2, v3, v4):
        v.wait_send()
    for cp in stores:
        cp.wait()


def on_device(
    entities, panel_rows, relations, source_owner, source_row, relation_ids, target_ids, negatives
):
    dma, vm = pltpu.SemaphoreType.DMA, pltpu.VMEM
    scratch = [
        vm((2 * DP, ROWS), BF16),
        vm((DEV, 128), F32), vm((DEV, 16), F32), vm((DEV, 16), F32),
        vm((DEV, 128), F32), vm((DEV, 128), F32), vm((DEV, 128), F32),
        vm((4, 4, D, PANEL), F32), vm((KC, ROWS), BF16),
        vm((DP, 256), BF16), vm((DP, 256), BF16), vm((NI, PANEL), F32),
        vm((2, DEV * MSG, 128), F32), vm((2, DEV * MSG, 128), F32),
        vm((2, DEV * MSG, 128), F32), vm((SLOTS, DP), F32),
        vm((SLOTS, 128), I32), vm((SLOTS, 128), I32),
        vm((BM, ROWS), F32), vm((BM, KC), BF16),
        vm((SLOTS, ROWS), BF16), vm((SLOTS, ROWS), BF16), vm((DP, 256), F32),
        vm((3, 4, HALF, PANEL), F32), vm((3, 4, HALF, PANEL), F32),
        vm((4, HALF, PANEL), F32), vm((4, HALF, PANEL), F32),
        vm((3, HALF, PANEL), F32), vm((3, HALF, PANEL), F32),
        vm((NO, 64, 256), F32), vm((NI, 8, 128), F32), vm((NI, 8, 128), F32),
        vm((8, 128), F32), vm((NI, 8, 128), F32), vm((NO, 64, 256), F32),
        dma((14,)),
        dma, dma, dma, dma,
        dma((2, 3)), dma((2, 3)), dma((2, 4, 3)), dma((2, 4, 3)),
        dma((2,)), dma((2,)), dma((2,)), dma((2,)),
        dma((2, 3)), dma((2, 3)), dma((2, 3)), dma((2, 3)),
        dma, dma, dma, dma, dma, dma, dma, dma,
    ]
    vmem = pl.BlockSpec(memory_space=pltpu.VMEM)
    anyw = pl.BlockSpec(memory_space=pl.ANY)
    entity, panel, relation = pl.pallas_call(
        step_kernel,
        out_shape=(
            jax.ShapeDtypeStruct((D, ROWS), F32),
            jax.ShapeDtypeStruct((D, PANEL), F32),
            jax.ShapeDtypeStruct((D, RELS), F32),
        ),
        in_specs=[anyw] + [vmem] * 7,
        out_specs=(anyw, vmem, vmem),
        scratch_shapes=scratch,
        compiler_params=pltpu.CompilerParams(
            collective_id=0, has_side_effects=True, vmem_limit_bytes=61 * 2**20
        ),
        name="edge_step",
    )(
        entities.T, panel_rows.T, relations.T,
        source_owner.reshape(1, EDGES), source_row.reshape(1, EDGES),
        relation_ids.reshape(1, EDGES), target_ids.reshape(1, EDGES), negatives,
    )
    return entity.T, panel.T, relation.T


def solution(mesh):
    placed = (
        P(("outer", "inner"), None),
        P(("outer", "inner"), None),
        P(),
        P(("outer", "inner")),
        P(("outer", "inner")),
        P(("outer", "inner")),
        P(("outer", "inner")),
        P(("outer", "inner"), None),
    )
    return jax.shard_map(
        on_device,
        mesh=mesh,
        in_specs=placed,
        out_specs=(P(("outer", "inner"), None), P(("outer", "inner"), None), P()),
        check_vma=False,
    )
```
